256 devices in a mesh: rows: 64 (over x, z, core), cols: 4 (over y).
Axes of the slice: x: 4, y: 4, z: 8, core: 2. Of those that a mesh axis runs over, the one named last changes fastest.
Arguments:
- kernel: float32 [16384, 16384], P('rows', 'cols'), may hold values from 0 to 2, as said below
- row_block: int32 [256], P('rows'), may hold values from 0 to 255, as said below
- panel_order: int32 [2], replicated, may hold values from 0 to 63, as said below
- samples: float32 [16384, 512], P('rows', 'cols'), may hold values from -6 to 6
Outputs:
- trailing: float32 [16384, 16384], P('rows', 'cols')
- factor: float32 [16384, 512], P('rows')
- solved: float32 [512, 512], P(None, 'cols')
- reduced_samples: float32 [16384, 512], P('rows', 'cols')
The draws below stay inside these ranges and needn't reach their ends.
Inputs may be any that keep to these rules, and one draw needn't show every extreme that they name: `row_block`: the stored row blocks of rows index i (stored blocks i * 4 to (i + 1) * 4 - 1) hold the global row blocks i + t * 64, t = 0 .. 3, each once, in some order. `panel_order`: the entries are distinct, and one of them is 63. `kernel`: in global row order the matrix is symmetric and positive definite, its smallest eigenvalue 0.25 or more.
All inputs are finite; a program needn't handle non-finite values.
Results may differ from the reference program's by a relative error of at most 0.0003.
Values sent between devices are 32-bit elements; how exact they have to be, the bound alone decides.
No kernel may reach another device: no remote copies, remote signals or barrier semaphores. Data moves between devices by JAX's collectives and lax.ppermute only.
A program may use at most 128 MiB of HBM per device.

```python
import jax
import jax.numpy as jnp
from jax import lax

N = 16384
SAMPLES = 512
PW = 256
PANELS = 2
NBLK = 256
BPD = 4
NPB = 64


def block_layout(key):
    devices_rows = NBLK // BPD
    scores = jax.random.randint(jax.random.fold_in(key, 7), (devices_rows, BPD), 0, 1 << 20) * BPD
    scores = scores + jnp.arange(BPD, dtype=jnp.int32)[None, :]
    ranking = jnp.argsort(scores, axis=1).astype(jnp.int32)
    layout = jnp.arange(devices_rows, dtype=jnp.int32)[:, None] + devices_rows * ranking
    return layout.reshape(NBLK).astype(jnp.int32)


def draw_row_block(key, part):
    return block_layout(key)


def draw_panel_order(key, part):
    others = jax.random.permutation(jax.random.fold_in(key, 11), NPB - 1)[:PANELS - 1].astype(jnp.int32)
    joined = jnp.concatenate([jnp.full((1,), NPB - 1, jnp.int32), others], 0)
    place = jax.random.randint(jax.random.fold_in(key, 17), (), 0, PANELS)
    return jnp.roll(joined, place).astype(jnp.int32)


def draw_kernel(key, part):
    layout = block_layout(key)
    sites_key = jax.random.fold_in(key, 13)
    spots = jax.random.uniform(sites_key, (N, 2), jnp.float32)
    length_scale = 0.15
    nugget = 0.3
    block_rows = N // NBLK
    rows_at = (layout[:, None] * block_rows + jnp.arange(block_rows, dtype=jnp.int32)[None, :]).reshape(N)
    here = spots[rows_at]
    delta_x = here[:, 0:1] - spots[None, :, 0]
    delta_y = here[:, 1:2] - spots[None, :, 1]
    distance = jnp.sqrt(delta_x * delta_x + delta_y * delta_y)
    cover = jnp.exp(-distance / length_scale)
    same_site = (rows_at[:, None] == jnp.arange(N, dtype=jnp.int32)[None, :]).astype(jnp.float32)
    return (cover + nugget * same_site).astype(jnp.float32)


def steps_of(key, dims, split, low, high):
    level = 1.0
    for dim, parts in split:
        heights = jax.random.uniform(jax.random.fold_in(jax.random.fold_in(key, 6), dim), (parts,), jnp.float32, low / len(split), high / len(split))
        level = level * jnp.repeat(jnp.exp(heights), dims[dim] // parts).reshape((-1,) + (1,) * (len(dims) - 1 - dim))
    return level


def scatter_about(key, dims, deviation, bound, split=(), kind=jnp.bfloat16):
    entries = jax.random.normal(key, dims, jnp.float32) * deviation
    if len(split) > 0:
        entries = steps_of(key, dims, split, -0.22, 0.18) * entries
    return jnp.clip(entries, min=-bound, max=bound).astype(kind)


def setup_inputs(seed: int = 0) -> dict:
    key_list = jax.random.split(jax.random.key(seed), 5)
    kernel = draw_kernel(jax.random.fold_in(key_list[4], 71), 0)
    row_block = draw_row_block(jax.random.fold_in(key_list[4], 71), 0)
    panel_order = draw_panel_order(jax.random.fold_in(key_list[4], 71), 0)
    samples = scatter_about(key_list[3], (N, SAMPLES), 1.0, 6.0, ((0, 64), (1, 4)), jnp.float32)
    return dict(kernel=kernel, row_block=row_block, panel_order=panel_order, samples=samples)


EXACT = lax.Precision.HIGHEST

def to_global(array, row_block):
    blocks_all = row_block.shape[0]
    ranking = jnp.argsort(row_block).astype(jnp.int32)
    return jnp.take(array.reshape(blocks_all, -1, array.shape[1]), ranking, axis=0).reshape(array.shape)

def to_stored(array, row_block):
    blocks_all = row_block.shape[0]
    return jnp.take(array.reshape(blocks_all, -1, array.shape[1]), row_block, axis=0).reshape(array.shape)

def times_transposed(left_side, right_side):
    return lax.dot_general(left_side.astype(jnp.float32), right_side.astype(jnp.float32), (((1,), (1,)), ((), ())), precision=EXACT, preferred_element_type=jnp.float32)

def matmul_plain(left_side, right_side):
    return jnp.dot(left_side.astype(jnp.float32), right_side.astype(jnp.float32), precision=EXACT, preferred_element_type=jnp.float32)

def reference(kernel, row_block, panel_order, samples):
    matrix = to_global(kernel, row_block)
    right_side = to_global(samples, row_block)
    identity = jnp.eye(PW, dtype=jnp.float32)
    factors = []
    solutions = []
    for panel_step in range(PANELS):
        panel_start = (panel_order[panel_step] * PW).astype(jnp.int32)
        columns = lax.dynamic_slice_in_dim(matrix, panel_start, PW, 1)
        diagonal = lax.dynamic_slice_in_dim(columns, panel_start, PW, 0)
        lower_factor = jnp.linalg.cholesky(diagonal)
        inverse = jax.scipy.linalg.solve_triangular(lower_factor, identity, lower=True)
        factor_now = times_transposed(columns, inverse)
        panel_right = lax.dynamic_slice_in_dim(right_side, panel_start, PW, 0)
        solved_now = matmul_plain(inverse, panel_right)
        right_side = right_side - matmul_plain(factor_now, solved_now)
        matrix = matrix - times_transposed(factor_now, factor_now)
        factors.append(factor_now)
        solutions.append(solved_now)
    factor_all = jnp.concatenate(factors, 1)
    return (to_stored(matrix, row_block), to_stored(factor_all, row_block), jnp.concatenate(solutions, 0), to_stored(right_side, row_block))
```

```python
import jax
import jax.numpy as jnp
from jax import lax
from jax.experimental import pallas as pl
from jax.experimental.pallas import tpu as pltpu
from jax.sharding import PartitionSpec as P

PW = 256
PANELS = 2
EXACT = lax.Precision.HIGHEST
SIDE = 128
STEP = 8


def dot_nt(a, b, precision=EXACT):
    return lax.dot_general(a, b, (((1,), (1,)), ((), ())), precision=precision, preferred_element_type=jnp.float32)


def dot_nn(a, b, precision=EXACT):
    return lax.dot_general(a, b, (((1,), (0,)), ((), ())), precision=precision, preferred_element_type=jnp.float32)


def lanes_of(rows, lane):
    return jnp.broadcast_to(rows[:, lane : lane + 1], (STEP, SIDE))


def sublanes_of(rows, sub):
    return jnp.broadcast_to(rows[sub : sub + 1, :], (STEP, SIDE))


def small_inverse(spread):
    inv, low = [None] * STEP, [[None] * STEP for _ in range(STEP)]
    rest = [list(r) for r in spread]
    for s in range(STEP):
        inv[s] = lax.rsqrt(rest[s][s])
        for r in range(s + 1, STEP):
            low[r][s] = rest[r][s] * inv[s]
        for r in range(s + 1, STEP):
            for q in range(s + 1, r + 1):
                rest[r][q] = rest[r][q] - low[r][s] * low[q][s]
    out = [[None] * STEP for _ in range(STEP)]
    for r in range(STEP):
        out[r][r] = inv[r]
        for s in range(r):
            total = low[r][s] * out[s][s]
            for q in range(s + 1, r):
                total = total + low[r][q] * out[q][s]
            out[r][s] = -inv[r] * total
    return out


def tile_inverse(d_ref, x_ref):
    groups = SIDE // STEP
    sub = lax.broadcasted_iota(jnp.int32, (STEP, SIDE), 0)
    lane = lax.broadcasted_iota(jnp.int32, (STEP, SIDE), 1)
    left = [d_ref[STEP * g : STEP * (g + 1), :] for g in range(groups)]
    right = [jnp.where(lane == sub + STEP * g, 1.0, 0.0).astype(jnp.float32) for g in range(groups)]
    for b in range(groups):
        here_l, here_r = left[b], right[b]
        cols = [lanes_of(here_l, STEP * b + s) for s in range(STEP)]
        spread = [[sublanes_of(cols[s], r) if s <= r else None for s in range(STEP)] for r in range(STEP)]
        v = small_inverse(spread)
        in_l = [sublanes_of(here_l, s) for s in range(STEP)]
        in_r = [sublanes_of(here_r, s) for s in range(STEP)]
        out_l, out_r = [], []
        for r in range(STEP):
            tl, tr = v[r][0] * in_l[0], v[r][0] * in_r[0]
            for s in range(1, r + 1):
                tl, tr = tl + v[r][s] * in_l[s], tr + v[r][s] * in_r[s]
            out_l.append(tl)
            out_r.append(tr)
        new_r = out_r[0]
        for r in range(1, STEP):
            new_r = jnp.where(sub == r, out_r[r], new_r)
        x_ref[STEP * b : STEP * (b + 1), :] = new_r
        if b + 1 == groups:
            break
        t_l, t_r = [], []
        for s in range(STEP):
            tl, tr = v[STEP - 1][s] * out_l[STEP - 1], v[STEP - 1][s] * out_r[STEP - 1]
            for r in range(s, STEP - 1):
                tl, tr = tl + v[r][s] * out_l[r], tr + v[r][s] * out_r[r]
            t_l.append(tl)
            t_r.append(tr)
        for g in range(b + 1, groups):
            c = [lanes_of(left[g], STEP * b + s) for s in range(STEP)]
            sl, sr = c[0] * t_l[0], c[0] * t_r[0]
            for s in range(1, STEP):
                sl, sr = sl + c[s] * t_l[s], sr + c[s] * t_r[s]
            left[g], right[g] = left[g] - sl, right[g] - sr


def factor_kernel(a_ref, p_ref, rc_ref, ri_ref, f_ref, w_ref, y_ref, r_ref, a, v, d, x):
    size = a.shape[0]
    tiles = size // SIDE
    a[...] = a_ref[...]
    v[...] = jnp.zeros_like(v)

    @pl.loop(0, tiles)
    def _(k):
        at = pl.multiple_of(k * SIDE, SIDE)
        d[...] = a[pl.ds(at, SIDE), pl.ds(at, SIDE)]
        tile_inverse(d, x)
        for step in range(tiles):
            @pl.when(k == step)
            def _():
                lo, hi = step * SIDE, (step + 1) * SIDE
                own = x[...]
                v[lo:hi, lo:hi] = own
                if step:
                    v[lo:hi, :lo] = dot_nn(own, v[lo:hi, :lo])
                if hi < size:
                    below = dot_nt(a[hi:, lo:hi], own)
                    a[hi:, hi:] = a[hi:, hi:] - dot_nt(below, below)
                    v[hi:, :hi] = v[hi:, :hi] - dot_nn(below, v[lo:hi, :hi])

    f = dot_nt(p_ref[...], v[...])
    f_ref[...] = f
    y = dot_nn(v[...], rc_ref[...])
    y_ref[...] = y
    r_ref[...] = ri_ref[...] - dot_nn(f, y)
    w_ref[...] = dot_nn(f, v[...])


def factor_call(a, p, rc, ri):
    size, rows, right = a.shape[0], p.shape[0], rc.shape[1]
    f32 = jnp.float32
    return pl.pallas_call(
        factor_kernel,
        out_shape=[
            jax.ShapeDtypeStruct((rows, size), f32),
            jax.ShapeDtypeStruct((rows, size), f32),
            jax.ShapeDtypeStruct((size, right), f32),
            jax.ShapeDtypeStruct((rows, right), f32),
        ],
        scratch_shapes=[
            pltpu.VMEM((size, size), f32),
            pltpu.VMEM((size, size), f32),
            pltpu.VMEM((SIDE, SIDE), f32),
            pltpu.VMEM((SIDE, SIDE), f32),
        ],
        compiler_params=pltpu.CompilerParams(vmem_limit_bytes=40 * 1024 * 1024),
        name="factor",
    )(a, p, rc, ri)


def pick(choices, index):
    out = choices[0]
    for at in range(1, len(choices)):
        out = jnp.where(index == at, choices[at], out)
    return out


def on_device(kernel, row_block, panel_order, samples):
    rows_count, cols_count = lax.axis_size("rows"), lax.axis_size("cols")
    row_place, col_place = lax.axis_index("rows"), lax.axis_index("cols")
    blocks_here = row_block.shape[0]
    local_rows, local_cols = kernel.shape
    block_rows = local_rows // blocks_here
    right_cols = samples.shape[1]
    part_rows = block_rows // cols_count
    chunks = PANELS * PW // SIDE

    strata = row_block // rows_count
    slots = [
        jnp.sum(jnp.where(strata == t, jnp.arange(blocks_here, dtype=jnp.int32), 0))
        for t in range(blocks_here)
    ]
    slots = jnp.stack(slots)
    owners, x_at, z_at, own = [], [], [], []
    for k in range(PANELS):
        panel = panel_order[k]
        owner = panel * PW // local_cols
        inside = panel % (local_cols // PW)
        owners.append(owner)
        x_at.append(inside // 4)
        z_at.append(inside % 4)
        own.append(lax.dynamic_slice_in_dim(kernel, inside * PW, PW, 1))
    own = jnp.concatenate(own, 1)

    def message(to):
        parts = [lax.dynamic_slice_in_dim(own, slots[to] * block_rows, block_rows, 0)]
        for k in range(PANELS):
            parts.append(
                lax.dynamic_slice_in_dim(
                    own, slots[owners[k]] * block_rows + to * part_rows, part_rows, 0
                )
            )
        return jnp.concatenate(parts, 0)

    def col_ring(shift):
        return [(i, (i + shift) % cols_count) for i in range(cols_count)]

    got = []
    for shift in range(cols_count):
        sent = message((col_place + shift) % cols_count)
        got.append(lax.ppermute(sent, "cols", col_ring(shift)) if shift else sent)
    mine = jnp.concatenate(
        [
            pick([g[:, k * PW : (k + 1) * PW] for g in got], (col_place - owners[k]) % cols_count)
            for k in range(PANELS)
        ],
        1,
    )
    piece = mine[:block_rows]
    across = lax.all_gather(piece, "rows", axis=0, tiled=True)

    load = []
    for k in range(PANELS):
        share = mine[block_rows + k * part_rows : block_rows + (k + 1) * part_rows]
        load += [share[:, c * SIDE : (c + 1) * SIDE] for c in range(chunks)]
        load.append(lax.dynamic_slice_in_dim(samples, slots[owners[k]] * block_rows, block_rows, 0))
    load = jnp.concatenate(load, 0).reshape(PANELS, 2 * block_rows, SIDE)

    def row_pairs(move):
        pairs = []
        for r in range(rows_count):
            x, z, core = move(r // 16, r % 16 // 2, r % 2)
            pairs.append((r, x % 4 * 16 + z % 8 * 2 + core))
        return pairs

    def spread(load, pairs_of, place, at):
        came = [load] + [lax.ppermute(load, "rows", pairs_of(s)) for s in range(1, 4)]
        return jnp.stack([pick([c[k] for c in came], (place - at[k]) % 4) for k in range(PANELS)])

    load = spread(load, lambda s: row_pairs(lambda x, z, c: (x + s, z, c)), row_place // 16, x_at)
    load = spread(
        load, lambda s: row_pairs(lambda x, z, c: (x, z + 2 * s, c)), row_place % 16 // 4, z_at
    )
    other = lax.ppermute(load, "rows", row_pairs(lambda x, z, c: (x, z ^ 1, c)))
    odd = row_place // 2 % 2 == 1
    load = jnp.stack([jnp.where(odd, other, load), jnp.where(odd, load, other)])
    square, right = load[:, :, :block_rows], load[:, :, block_rows:]
    came = [square] + [lax.ppermute(square, "cols", col_ring(s)) for s in range(1, cols_count)]
    square = [pick(came, (col_place - to) % cols_count) for to in range(cols_count)]
    load = jnp.stack(square + [right])
    other = lax.ppermute(load, "rows", row_pairs(lambda x, z, c: (x, z, c ^ 1)))
    odd = row_place % 2 == 1
    load = jnp.stack([jnp.where(odd, other, load), jnp.where(odd, load, other)])
    right = load[:, cols_count].transpose(2, 1, 0, 3, 4).reshape(PANELS * PW, right_cols)
    square = load[:, :cols_count].reshape(2, cols_count, 2, PANELS, chunks, part_rows, SIDE)
    square = square.transpose(3, 2, 0, 1, 5, 4, 6).reshape(PANELS * PW, PANELS * PW)

    came = [piece] + [lax.ppermute(piece, "cols", col_ring(s)) for s in range(1, cols_count)]
    here = jnp.concatenate(
        [pick(came, (col_place - strata[u]) % cols_count) for u in range(blocks_here)], 0
    )
    factor, weights, solved, reduced = factor_call(square, here, right, samples)
    trailing = kernel - dot_nt(weights, across, lax.Precision.HIGH)
    return trailing, factor, solved, reduced


def solution(mesh):
    in_specs = (P("rows", "cols"), P("rows"), P(), P("rows", "cols"))
    out_specs = (P("rows", "cols"), P("rows", None), P(None, "cols"), P("rows", "cols"))
    return jax.shard_map(
        on_device, mesh=mesh, in_specs=in_specs, out_specs=out_specs, check_vma=False
    )
```

```python
import jax
import jax.numpy as jnp
from jax import lax
from jax.experimental import pallas as pl
from jax.experimental.pallas import tpu as pltpu
from jax.sharding import PartitionSpec as P

PW = 256
PANELS = 2
EXACT = lax.Precision.HIGHEST
SIDE = 128
STEP = 8


def dot_nt(a, b, precision=EXACT):
    return lax.dot_general(a, b, (((1,), (1,)), ((), ())), precision=precision, preferred_element_type=jnp.float32)


def dot_nn(a, b, precision=EXACT):
    return lax.dot_general(a, b, (((1,), (0,)), ((), ())), precision=precision, preferred_element_type=jnp.float32)


def lanes_of(rows, lane):
    return jnp.broadcast_to(rows[:, lane : lane + 1], (STEP, SIDE))


def sublanes_of(rows, sub):
    return jnp.broadcast_to(rows[sub : sub + 1, :], (STEP, SIDE))


def small_inverse(spread):
    inv, low = [None] * STEP, [[None] * STEP for _ in range(STEP)]
    rest = [list(r) for r in spread]
    for s in range(STEP):
        inv[s] = lax.rsqrt(rest[s][s])
        for r in range(s + 1, STEP):
            low[r][s] = rest[r][s] * inv[s]
        for r in range(s + 1, STEP):
            for q in range(s + 1, r + 1):
                rest[r][q] = rest[r][q] - low[r][s] * low[q][s]
    out = [[None] * STEP for _ in range(STEP)]
    for r in range(STEP):
        out[r][r] = inv[r]
        for s in range(r):
            total = low[r][s] * out[s][s]
            for q in range(s + 1, r):
                total = total + low[r][q] * out[q][s]
            out[r][s] = -inv[r] * total
    return out


def tile_inverse(d_ref, x_ref):
    groups = SIDE // STEP
    sub = lax.broadcasted_iota(jnp.int32, (STEP, SIDE), 0)
    lane = lax.broadcasted_iota(jnp.int32, (STEP, SIDE), 1)
    left = [d_ref[STEP * g : STEP * (g + 1), :] for g in range(groups)]
    right = [jnp.where(lane == sub + STEP * g, 1.0, 0.0).astype(jnp.float32) for g in range(groups)]
    for b in range(groups):
        here_l, here_r = left[b], right[b]
        cols = [lanes_of(here_l, STEP * b + s) for s in range(STEP)]
        spread = [[sublanes_of(cols[s], r) if s <= r else None for s in range(STEP)] for r in range(STEP)]
        v = small_inverse(spread)
        in_l = [sublanes_of(here_l, s) for s in range(STEP)]
        in_r = [sublanes_of(here_r, s) for s in range(STEP)]
        out_l, out_r = [], []
        for r in range(STEP):
            tl, tr = v[r][0] * in_l[0], v[r][0] * in_r[0]
            for s in range(1, r + 1):
                tl, tr = tl + v[r][s] * in_l[s], tr + v[r][s] * in_r[s]
            out_l.append(tl)
            out_r.append(tr)
        new_r = out_r[0]
        for r in range(1, STEP):
            new_r = jnp.where(sub == r, out_r[r], new_r)
        x_ref[STEP * b : STEP * (b + 1), :] = new_r
        if b + 1 == groups:
            break
        t_l, t_r = [], []
        for s in range(STEP):
            tl, tr = v[STEP - 1][s] * out_l[STEP - 1], v[STEP - 1][s] * out_r[STEP - 1]
            for r in range(s, STEP - 1):
                tl, tr = tl + v[r][s] * out_l[r], tr + v[r][s] * out_r[r]
            t_l.append(tl)
            t_r.append(tr)
        for g in range(b + 1, groups):
            c = [lanes_of(left[g], STEP * b + s) for s in range(STEP)]
            sl, sr = c[0] * t_l[0], c[0] * t_r[0]
            for s in range(1, STEP):
                sl, sr = sl + c[s] * t_l[s], sr + c[s] * t_r[s]
            left[g], right[g] = left[g] - sl, right[g] - sr


def inverse_kernel(a_ref, v, a, d, x):
    size = a.shape[0]
    tiles = size // SIDE
    a[...] = a_ref[...]
    v[...] = jnp.zeros_like(v)

    @pl.loop(0, tiles)
    def _(k):
        at = pl.multiple_of(k * SIDE, SIDE)
        d[...] = a[pl.ds(at, SIDE), pl.ds(at, SIDE)]
        tile_inverse(d, x)
        for step in range(tiles):

            @pl.when(k == step)
            def _():
                lo, hi = step * SIDE, (step + 1) * SIDE
                own = x[...]
                v[lo:hi, lo:hi] = own
                if step:
                    v[lo:hi, :lo] = dot_nn(own, v[lo:hi, :lo])
                if hi < size:
                    below = dot_nt(a[hi:, lo:hi], own)
                    a[hi:, hi:] = a[hi:, hi:] - dot_nt(below, below)
                    v[hi:, :hi] = v[hi:, :hi] - dot_nn(below, v[lo:hi, :hi])


def inverse_call(a):
    size = a.shape[0]
    return pl.pallas_call(
        inverse_kernel,
        out_shape=jax.ShapeDtypeStruct((size, size), jnp.float32),
        scratch_shapes=[
            pltpu.VMEM((size, size), jnp.float32),
            pltpu.VMEM((SIDE, SIDE), jnp.float32),
            pltpu.VMEM((SIDE, SIDE), jnp.float32),
        ],
        cost_estimate=pl.CostEstimate(flops=20_000_000_000, bytes_accessed=2_000_000, transcendentals=0),
        compiler_params=pltpu.CompilerParams(vmem_limit_bytes=16 * 1024 * 1024),
        name="factor_inverse",
    )(a)


def apply_kernel(v_ref, p_ref, rc_ref, ri_ref, f_ref, wh_ref, wl_ref, y_ref, r_ref):
    v = v_ref[...]
    f = dot_nt(p_ref[...], v)
    f_ref[...] = f
    y = dot_nn(v, rc_ref[...])
    y_ref[...] = y
    r_ref[...] = ri_ref[...] - dot_nn(f, y)
    wh_ref[...], wl_ref[...] = halves(dot_nn(f, v))


def halves(array):
    high = array.astype(jnp.bfloat16)
    return high, (array - high.astype(jnp.float32)).astype(jnp.bfloat16)


def apply_call(v, p, rc, ri):
    size, rows, right = v.shape[0], p.shape[0], rc.shape[1]
    f32 = jnp.float32
    return pl.pallas_call(
        apply_kernel,
        out_shape=[
            jax.ShapeDtypeStruct((rows, size), f32),
            jax.ShapeDtypeStruct((rows, size), jnp.bfloat16),
            jax.ShapeDtypeStruct((rows, size), jnp.bfloat16),
            jax.ShapeDtypeStruct((size, right), f32),
            jax.ShapeDtypeStruct((rows, right), f32),
        ],
        cost_estimate=pl.CostEstimate(flops=2_000_000_000, bytes_accessed=4_000_000, transcendentals=0),
        compiler_params=pltpu.CompilerParams(vmem_limit_bytes=16 * 1024 * 1024),
        name="apply_factor",
    )(v, p, rc, ri)


def update_kernel(k_ref, wh_ref, wl_ref, b_ref, o_ref):
    high, low = halves(b_ref[...])
    wh, wl = wh_ref[...], wl_ref[...]
    total = dot_nt(wh, high, None) + dot_nt(wh, low, None) + dot_nt(wl, high, None)
    o_ref[...] = k_ref[...] - total


def update_call(kernel, wh, wl, across):
    rows, cols = kernel.shape
    size = wh.shape[1]
    width = 512
    return pl.pallas_call(
        update_kernel,
        grid=(cols // width,),
        in_specs=[
            pl.BlockSpec((rows, width), lambda i: (0, i)),
            pl.BlockSpec((rows, size), lambda i: (0, 0)),
            pl.BlockSpec((rows, size), lambda i: (0, 0)),
            pl.BlockSpec((width, size), lambda i: (i, 0)),
        ],
        out_specs=pl.BlockSpec((rows, width), lambda i: (0, i)),
        out_shape=jax.ShapeDtypeStruct((rows, cols), jnp.float32),
        cost_estimate=pl.CostEstimate(flops=6 * rows * cols * size, bytes_accessed=16_000_000, transcendentals=0),
        compiler_params=pltpu.CompilerParams(vmem_limit_bytes=60 * 1024 * 1024),
        name="trailing_update",
    )(kernel, wh, wl, across)


def pack_kernel(order_ref, block_ref, kernel_ref, samples_ref, *rest):
    messages, right_ref, own, sems = rest[:-3], rest[-3], rest[-2], rest[-1]
    strata = len(messages)
    me = lax.axis_index("cols")
    local_cols = kernel_ref.shape[1]
    blocks_here = strata
    block_rows = kernel_ref.shape[0] // blocks_here
    part_rows = block_rows // strata
    per_place = local_cols // PW
    copies = []
    for k in range(PANELS):
        at = pl.multiple_of(lax.rem(order_ref[k], per_place) * PW, PW)
        copies.append(
            pltpu.make_async_copy(
                kernel_ref.at[:, pl.ds(at, PW)], own.at[:, k * PW : (k + 1) * PW], sems.at[k]
            )
        )
        copies[-1].start()
    rows_count = lax.axis_size("rows")

    def start_of(stratum):
        slot = jnp.int32(0)
        for u in range(blocks_here):
            slot = jnp.where(lax.div(block_ref[u], rows_count) == stratum, u, slot)
        return slot * block_rows

    starts = [start_of(lax.div(order_ref[k], per_place)) for k in range(PANELS)]
    for k in range(PANELS):
        right_ref[k] = samples_ref[pl.ds(pl.multiple_of(starts[k], block_rows), block_rows), :]
    for copy in copies:
        copy.wait()
    for shift in range(strata):
        to = (me + shift) & (strata - 1)
        out = messages[shift]
        out[:block_rows] = own[pl.ds(pl.multiple_of(start_of(to), block_rows), block_rows), :]
        for k in range(PANELS):
            lo = block_rows + k * part_rows
            at = pl.multiple_of(starts[k] + to * part_rows, part_rows)
            out[lo : lo + part_rows] = own[pl.ds(at, part_rows), :]


def pack_call(panel_order, row_block, kernel, samples):
    strata = lax.axis_size("cols")
    rows, right = samples.shape
    block_rows = rows // row_block.shape[0]
    size = PANELS * PW
    f32 = jnp.float32
    message = jax.ShapeDtypeStruct((block_rows + PANELS * (block_rows // strata), size), f32)
    *messages, picked = pl.pallas_call(
        pack_kernel,
        in_specs=[
            pl.BlockSpec(memory_space=pltpu.SMEM),
            pl.BlockSpec(memory_space=pltpu.SMEM),
            pl.BlockSpec(memory_space=pltpu.HBM),
            pl.BlockSpec(memory_space=pltpu.VMEM),
        ],
        out_shape=[message] * strata + [jax.ShapeDtypeStruct((PANELS, block_rows, right), f32)],
        scratch_shapes=[pltpu.VMEM((rows, size), f32), pltpu.SemaphoreType.DMA((PANELS,))],
        cost_estimate=pl.CostEstimate(flops=0, bytes_accessed=2_000_000, transcendentals=0),
        compiler_params=pltpu.CompilerParams(vmem_limit_bytes=60 * 1024 * 1024),
        name="pack_messages",
    )(panel_order, row_block, kernel, samples)
    return messages, picked


def pick(choices, index):
    out = choices[0]
    for at in range(1, len(choices)):
        out = jnp.where(index == at, choices[at], out)
    return out


def on_device(kernel, row_block, panel_order, samples):
    rows_count, cols_count = lax.axis_size("rows"), lax.axis_size("cols")
    row_place, col_place = lax.axis_index("rows"), lax.axis_index("cols")
    blocks_here = row_block.shape[0]
    local_rows, local_cols = kernel.shape
    block_rows = local_rows // blocks_here
    right_cols = samples.shape[1]
    part_rows = block_rows // cols_count
    chunks = PANELS * PW // SIDE
    per_place = local_cols // PW

    owners = [lax.div(panel_order[k], per_place) for k in range(PANELS)]
    x_at = [lax.div(lax.rem(panel_order[k], per_place), 4) for k in range(PANELS)]
    z_at = [lax.rem(panel_order[k], 4) for k in range(PANELS)]
    x_here, z_here = row_place >> 4, (row_place >> 2) & 3

    def col_ring(shift):
        return [(i, (i + shift) % cols_count) for i in range(cols_count)]

    def row_pairs(move):
        pairs = []
        for r in range(rows_count):
            x, z, core = move(r // 16, r % 16 // 2, r % 2)
            pairs.append((r, x % 4 * 16 + z % 8 * 2 + core))
        return pairs

    messages, right = pack_call(panel_order, row_block, kernel, samples)
    got = messages[:1] + [
        lax.ppermute(messages[s], "cols", col_ring(s)) for s in range(1, cols_count)
    ]
    mine = jnp.concatenate(
        [
            pick([g[:, k * PW : (k + 1) * PW] for g in got], (col_place - owners[k]) & (cols_count - 1))
            for k in range(PANELS)
        ],
        1,
    )
    piece = mine[:block_rows]
    across = lax.all_gather(piece, "rows", axis=0, tiled=True)

    load = []
    for k in range(PANELS):
        share = mine[block_rows + k * part_rows : block_rows + (k + 1) * part_rows]
        load += [share[:, c * SIDE : (c + 1) * SIDE] for c in range(chunks)]
        load.append(right[k])
    load = jnp.concatenate(load, 0).reshape(PANELS, 2 * block_rows, SIDE)
    came = [load] + [
        lax.ppermute(load, "rows", row_pairs(lambda x, z, c: (x + s, z, c))) for s in range(1, 4)
    ]
    load = jnp.stack([pick([c[k] for c in came], (x_here - x_at[k]) & 3) for k in range(PANELS)])
    piece, load = lax.optimization_barrier((piece, load))
    spread = [lax.ppermute(piece, "cols", col_ring(s)) for s in range(1, cols_count)]
    other = lax.ppermute(load, "rows", row_pairs(lambda x, z, c: (x, (z // 2 ^ 1) * 2 + z % 2, c)))
    load = jnp.stack(
        [jnp.where(z_at[k] == (z_here ^ 1), other[k], load[k]) for k in range(PANELS)]
    )
    *spread, load = lax.optimization_barrier((*spread, load))
    other = lax.ppermute(load, "rows", row_pairs(lambda x, z, c: (x, (3 - z // 2) * 2 + z % 2, c)))
    load = jnp.stack(
        [jnp.where((z_at[k] >> 1) != (z_here >> 1), other[k], load[k]) for k in range(PANELS)]
    )
    other = lax.ppermute(load, "rows", row_pairs(lambda x, z, c: (x, z ^ 1, c)))
    odd = (row_place & 2) != 0
    load = jnp.stack([jnp.where(odd, other, load), jnp.where(odd, load, other)])
    square, right = load[:, :, :block_rows], load[:, :, block_rows:]
    came = [square] + [lax.ppermute(square, "cols", col_ring(s)) for s in range(1, cols_count)]
    square = [pick(came, (col_place - to) & (cols_count - 1)) for to in range(cols_count)]
    load = jnp.stack(square + [right])
    other = lax.ppermute(load, "rows", row_pairs(lambda x, z, c: (x, z, c ^ 1)))
    odd = (row_place & 1) != 0
    load = jnp.stack([jnp.where(odd, other, load), jnp.where(odd, load, other)])
    right = load[:, cols_count].transpose(2, 1, 0, 3, 4).reshape(PANELS * PW, right_cols)
    square = load[:, :cols_count].reshape(2, cols_count, 2, PANELS, chunks, part_rows, SIDE)
    square = square.transpose(3, 2, 0, 1, 5, 4, 6).reshape(PANELS * PW, PANELS * PW)

    came = [piece] + spread
    strata = [lax.div(row_block[u], rows_count) for u in range(blocks_here)]
    here = jnp.concatenate(
        [pick(came, (col_place - strata[u]) & (cols_count - 1)) for u in range(blocks_here)], 0
    )
    factor, high, low, solved, reduced = apply_call(inverse_call(square), here, right, samples)
    trailing = update_call(kernel, high, low, across)
    return trailing, factor, solved, reduced


def solution(mesh):
    in_specs = (P("rows", "cols"), P("rows"), P(), P("rows", "cols"))
    out_specs = (P("rows", "cols"), P("rows", None), P(None, "cols"), P("rows", "cols"))
    return jax.shard_map(
        on_device, mesh=mesh, in_specs=in_specs, out_specs=out_specs, check_vma=False
    )
```

```python
import jax
import jax.numpy as jnp
from jax import lax
from jax.experimental import pallas as pl
from jax.experimental.pallas import tpu as pltpu
from jax.sharding import PartitionSpec as P

PW = 256
PANELS = 2
EXACT = lax.Precision.HIGHEST
SIDE = 128
STEP = 8


def dot_nt(a, b, precision=EXACT):
    return lax.dot_general(a, b, (((1,), (1,)), ((), ())), precision=precision, preferred_element_type=jnp.float32)


def dot_nn(a, b, precision=EXACT):
    return lax.dot_general(a, b, (((1,), (0,)), ((), ())), precision=precision, preferred_element_type=jnp.float32)


def lanes_of(rows, lane):
    return jnp.broadcast_to(rows[:, lane : lane + 1], (STEP, SIDE))


def sublanes_of(rows, sub):
    return jnp.broadcast_to(rows[sub : sub + 1, :], (STEP, SIDE))


def small_inverse(spread):
    inv, low = [None] * STEP, [[None] * STEP for _ in range(STEP)]
    rest = [list(r) for r in spread]
    for s in range(STEP):
        inv[s] = lax.rsqrt(rest[s][s])
        for r in range(s + 1, STEP):
            low[r][s] = rest[r][s] * inv[s]
        for r in range(s + 1, STEP):
            for q in range(s + 1, r + 1):
                rest[r][q] = rest[r][q] - low[r][s] * low[q][s]
    out = [[None] * STEP for _ in range(STEP)]
    for r in range(STEP):
        out[r][r] = inv[r]
        for s in range(r):
            total = low[r][s] * out[s][s]
            for q in range(s + 1, r):
                total = total + low[r][q] * out[q][s]
            out[r][s] = -inv[r] * total
    return out


def tile_inverse(d_ref, x_ref):
    groups = SIDE // STEP
    sub = lax.broadcasted_iota(jnp.int32, (STEP, SIDE), 0)
    lane = lax.broadcasted_iota(jnp.int32, (STEP, SIDE), 1)
    left = [d_ref[STEP * g : STEP * (g + 1), :] for g in range(groups)]
    right = [jnp.where(lane == sub + STEP * g, 1.0, 0.0).astype(jnp.float32) for g in range(groups)]
    for b in range(groups):
        here_l, here_r = left[b], right[b]
        cols = [lanes_of(here_l, STEP * b + s) for s in range(STEP)]
        spread = [[sublanes_of(cols[s], r) if s <= r else None for s in range(STEP)] for r in range(STEP)]
        v = small_inverse(spread)
        in_l = [sublanes_of(here_l, s) for s in range(STEP)]
        in_r = [sublanes_of(here_r, s) for s in range(STEP)]
        out_l, out_r = [], []
        for r in range(STEP):
            tl, tr = v[r][0] * in_l[0], v[r][0] * in_r[0]
            for s in range(1, r + 1):
                tl, tr = tl + v[r][s] * in_l[s], tr + v[r][s] * in_r[s]
            out_l.append(tl)
            out_r.append(tr)
        new_r = out_r[0]
        for r in range(1, STEP):
            new_r = jnp.where(sub == r, out_r[r], new_r)
        x_ref[STEP * b : STEP * (b + 1), :] = new_r
        if b + 1 == groups:
            break
        t_l, t_r = [], []
        for s in range(STEP):
            tl, tr = v[STEP - 1][s] * out_l[STEP - 1], v[STEP - 1][s] * out_r[STEP - 1]
            for r in range(s, STEP - 1):
                tl, tr = tl + v[r][s] * out_l[r], tr + v[r][s] * out_r[r]
            t_l.append(tl)
            t_r.append(tr)
        for g in range(b + 1, groups):
            c = [lanes_of(left[g], STEP * b + s) for s in range(STEP)]
            sl, sr = c[0] * t_l[0], c[0] * t_r[0]
            for s in range(1, STEP):
                sl, sr = sl + c[s] * t_l[s], sr + c[s] * t_r[s]
            left[g], right[g] = left[g] - sl, right[g] - sr


def halves(array):
    high = array.astype(jnp.bfloat16)
    return high, (array - high.astype(jnp.float32)).astype(jnp.bfloat16)


def two_tiles(a, v, d, x):
    v[...] = jnp.zeros_like(v)

    @pl.loop(0, 2)
    def _(k):
        at = pl.multiple_of(k * SIDE, SIDE)
        d[...] = a[pl.ds(at, SIDE), pl.ds(at, SIDE)]
        tile_inverse(d, x)

        @pl.when(k == 0)
        def _():
            own = x[...]
            v[:SIDE, :SIDE] = own
            below = dot_nt(a[SIDE:, :SIDE], own)
            a[SIDE:, SIDE:] = a[SIDE:, SIDE:] - dot_nt(below, below)
            v[SIDE:, :SIDE] = -dot_nn(below, own)

        @pl.when(k == 1)
        def _():
            own = x[...]
            v[SIDE:, SIDE:] = own
            v[SIDE:, :SIDE] = dot_nn(own, v[SIDE:, :SIDE])


def first_kernel(own_ref, other_ref, v_ref, rest_ref, under_ref, right_ref, a, top, d, x):
    row_place, col_place = lax.axis_index("rows"), lax.axis_index("cols")
    core, odd = row_place & 1, (row_place >> 1) & 1
    strata = own_ref.shape[0] - 1
    block_rows = own_ref.shape[3]
    part_rows = block_rows // strata
    for c, source in enumerate((own_ref, other_ref)):
        for z in range(2):
            member = (odd ^ z) * 2 + (core ^ c)
            for k in range(PANELS):
                base = k * PW + member * block_rows
                right_ref[pl.ds(pl.multiple_of(base, block_rows), block_rows), :] = source[strata, z, k]
                for shift in range(strata):
                    part = (col_place - shift) & (strata - 1)
                    at = pl.multiple_of(base + part * part_rows, part_rows)
                    for chunk in range(PANELS * PW // SIDE):
                        lo = chunk * part_rows
                        a[pl.ds(at, part_rows), chunk * SIDE : (chunk + 1) * SIDE] = source[
                            shift, z, k, lo : lo + part_rows
                        ]
    top[...] = a[:PW, :PW]
    two_tiles(top, v_ref, d, x)
    v = v_ref[...]
    low = dot_nt(a[PW:, :PW], v)
    rest_ref[...] = a[PW:, PW:] - dot_nt(low, low)
    under_ref[...] = -dot_nn(low, v)


def square(side):
    return jax.ShapeDtypeStruct((side, side), jnp.float32)


def first_call(own, other):
    right = jax.ShapeDtypeStruct((PANELS * PW, own.shape[-1]), jnp.float32)
    return pl.pallas_call(
        first_kernel,
        out_shape=[square(PW), square(PW), square(PW), right],
        scratch_shapes=[
            pltpu.VMEM((PANELS * PW, PANELS * PW), jnp.float32),
            pltpu.VMEM((PW, PW), jnp.float32),
            pltpu.VMEM((SIDE, SIDE), jnp.float32),
            pltpu.VMEM((SIDE, SIDE), jnp.float32),
        ],
        cost_estimate=pl.CostEstimate(flops=12_000_000_000, bytes_accessed=2_000_000, transcendentals=0),
        compiler_params=pltpu.CompilerParams(vmem_limit_bytes=16 * 1024 * 1024),
        name="eliminate_first",
    )(own, other)


def second_kernel(rest_ref, under_ref, v_ref, cross_ref, a, d, x):
    a[...] = rest_ref[...]
    two_tiles(a, v_ref, d, x)
    cross_ref[...] = dot_nn(v_ref[...], under_ref[...])


def second_call(rest, under):
    return pl.pallas_call(
        second_kernel,
        out_shape=[square(PW), square(PW)],
        scratch_shapes=[
            pltpu.VMEM((PW, PW), jnp.float32),
            pltpu.VMEM((SIDE, SIDE), jnp.float32),
            pltpu.VMEM((SIDE, SIDE), jnp.float32),
        ],
        cost_estimate=pl.CostEstimate(flops=12_000_000_000, bytes_accessed=2_000_000, transcendentals=0),
        compiler_params=pltpu.CompilerParams(vmem_limit_bytes=16 * 1024 * 1024),
        name="eliminate_second",
    )(rest, under)


def apply_kernel(block_ref, *refs):
    pieces, (v1_ref, cross_ref, v2_ref, rc_ref, ri_ref, f_ref, w_ref, y_ref, r_ref, p) = refs[:-10], refs[-10:]
    me = lax.axis_index("cols")
    rows_count = lax.axis_size("rows")
    block_rows = pieces[0].shape[0]
    for u in range(len(pieces)):
        shift = (me - lax.div(block_ref[u], rows_count)) & (len(pieces) - 1)
        for s, piece in enumerate(pieces):

            @pl.when(shift == s)
            def _():
                p[u * block_rows : (u + 1) * block_rows] = piece[...]

    v1, cross, v2 = v1_ref[...], cross_ref[...], v2_ref[...]
    p1, p2 = p[:, :PW], p[:, PW:]
    f1 = dot_nt(p1, v1)
    f2 = dot_nt(p1, cross) + dot_nt(p2, v2)
    f_ref[:, :PW] = f1
    f_ref[:, PW:] = f2
    w_ref[:, :PW] = dot_nn(f1, v1) + dot_nn(f2, cross)
    w_ref[:, PW:] = dot_nn(f2, v2)
    y1 = dot_nn(v1, rc_ref[:PW])
    y2 = dot_nn(cross, rc_ref[:PW]) + dot_nn(v2, rc_ref[PW:])
    y_ref[:PW] = y1
    y_ref[PW:] = y2
    r_ref[...] = ri_ref[...] - dot_nn(f1, y1) - dot_nn(f2, y2)


def apply_call(row_block, pieces, v1, cross, v2, rc, ri):
    size, right = rc.shape
    rows = ri.shape[0]
    f32 = jnp.float32
    operands = (*pieces, v1, cross, v2, rc, ri)
    return pl.pallas_call(
        apply_kernel,
        in_specs=[pl.BlockSpec(memory_space=pltpu.SMEM)]
        + [pl.BlockSpec(memory_space=pltpu.VMEM)] * len(operands),
        out_shape=[
            jax.ShapeDtypeStruct((rows, size), f32),
            jax.ShapeDtypeStruct((rows, size), f32),
            jax.ShapeDtypeStruct((size, right), f32),
            jax.ShapeDtypeStruct((rows, right), f32),
        ],
        scratch_shapes=[pltpu.VMEM((rows, size), f32)],
        cost_estimate=pl.CostEstimate(flops=4_000_000_000, bytes_accessed=4_000_000, transcendentals=0),
        compiler_params=pltpu.CompilerParams(vmem_limit_bytes=16 * 1024 * 1024),
        name="apply_factor",
    )(row_block, *operands)


WIDTH = 512


def update_kernel(moves, k_ref, w_ref, *refs):
    arrays, (o_ref, held, high, low, out, in_sems, out_sems) = refs[:-7], refs[-7:]
    cols = k_ref.shape[1]
    count = cols // WIDTH
    loads = [
        pltpu.make_async_copy(
            k_ref.at[:, i * WIDTH : (i + 1) * WIDTH], held.at[:, i * WIDTH : (i + 1) * WIDTH], in_sems.at[i]
        )
        for i in range(count)
    ]
    for load in loads:
        load.start()
    row_place = lax.axis_index("rows")
    block_rows = cols // lax.axis_size("rows")
    x, z, core = row_place >> 4, (row_place >> 1) & 7, row_place & 1
    for array, (dz, first, swapped) in zip(arrays, moves):
        for part in range(array.shape[0] // block_rows):
            place = ((x - first - part) & 3) * 16 + ((z - dz) & 7) * 2 + (core ^ swapped)
            at = pl.multiple_of(place * block_rows, block_rows)
            top, bottom = halves(array[part * block_rows : (part + 1) * block_rows])
            high[pl.ds(at, block_rows), :] = top
            low[pl.ds(at, block_rows), :] = bottom
    wh, wl = halves(w_ref[...])
    stores = []
    for i in range(count):
        at = slice(i * WIDTH, (i + 1) * WIDTH)
        top, bottom = high[at], low[at]
        total = dot_nt(wh, top, None) + dot_nt(wh, bottom, None) + dot_nt(wl, top, None)
        loads[i].wait()
        out[:, at] = held[:, at] - total
        stores.append(pltpu.make_async_copy(out.at[:, at], o_ref.at[:, at], out_sems.at[i]))
        stores[-1].start()
    for store in stores:
        store.wait()


def update_call(kernel, weights, arrays, moves):
    rows, cols = kernel.shape
    size = weights.shape[1]
    count = cols // WIDTH
    return pl.pallas_call(
        lambda *refs: update_kernel(moves, *refs),
        in_specs=[pl.BlockSpec(memory_space=pltpu.HBM)]
        + [pl.BlockSpec(memory_space=pltpu.VMEM)] * (1 + len(arrays)),
        out_specs=pl.BlockSpec(memory_space=pltpu.HBM),
        out_shape=jax.ShapeDtypeStruct((rows, cols), jnp.float32),
        scratch_shapes=[
            pltpu.VMEM((rows, cols), jnp.float32),
            pltpu.VMEM((cols, size), jnp.bfloat16),
            pltpu.VMEM((cols, size), jnp.bfloat16),
            pltpu.VMEM((rows, cols), jnp.float32),
            pltpu.SemaphoreType.DMA((count,)),
            pltpu.SemaphoreType.DMA((count,)),
        ],
        cost_estimate=pl.CostEstimate(flops=6 * rows * cols * size, bytes_accessed=16_000_000, transcendentals=0),
        compiler_params=pltpu.CompilerParams(vmem_limit_bytes=40 * 1024 * 1024),
        name="trailing_update",
    )(kernel, weights, *arrays)


def pack_kernel(order_ref, block_ref, kernel_ref, samples_ref, *rest):
    messages, right_ref, own, sems = rest[:-3], rest[-3], rest[-2], rest[-1]
    strata = len(messages)
    me = lax.axis_index("cols")
    local_cols = kernel_ref.shape[1]
    blocks_here = strata
    block_rows = kernel_ref.shape[0] // blocks_here
    part_rows = block_rows // strata
    per_place = local_cols // PW
    copies = []
    for k in range(PANELS):
        at = pl.multiple_of(lax.rem(order_ref[k], per_place) * PW, PW)
        copies.append(
            pltpu.make_async_copy(
                kernel_ref.at[:, pl.ds(at, PW)], own.at[:, k * PW : (k + 1) * PW], sems.at[k]
            )
        )
        copies[-1].start()
    rows_count = lax.axis_size("rows")

    def start_of(stratum):
        slot = jnp.int32(0)
        for u in range(blocks_here):
            slot = jnp.where(lax.div(block_ref[u], rows_count) == stratum, u, slot)
        return slot * block_rows

    starts = [start_of(lax.div(order_ref[k], per_place)) for k in range(PANELS)]
    for k in range(PANELS):
        right_ref[k] = samples_ref[pl.ds(pl.multiple_of(starts[k], block_rows), block_rows), :]
    for copy in copies:
        copy.wait()
    for shift in range(strata):
        to = (me + shift) & (strata - 1)
        out = messages[shift]
        out[:block_rows] = own[pl.ds(pl.multiple_of(start_of(to), block_rows), block_rows), :]
        for k in range(PANELS):
            lo = block_rows + k * part_rows
            at = pl.multiple_of(starts[k] + to * part_rows, part_rows)
            out[lo : lo + part_rows] = own[pl.ds(at, part_rows), :]


def pack_call(panel_order, row_block, kernel, samples):
    strata = lax.axis_size("cols")
    rows, right = samples.shape
    block_rows = rows // row_block.shape[0]
    size = PANELS * PW
    f32 = jnp.float32
    message = jax.ShapeDtypeStruct((block_rows + PANELS * (block_rows // strata), size), f32)
    *messages, picked = pl.pallas_call(
        pack_kernel,
        in_specs=[
            pl.BlockSpec(memory_space=pltpu.SMEM),
            pl.BlockSpec(memory_space=pltpu.SMEM),
            pl.BlockSpec(memory_space=pltpu.HBM),
            pl.BlockSpec(memory_space=pltpu.VMEM),
        ],
        out_shape=[message] * strata + [jax.ShapeDtypeStruct((PANELS, block_rows, right), f32)],
        scratch_shapes=[pltpu.VMEM((rows, size), f32), pltpu.SemaphoreType.DMA((PANELS,))],
        cost_estimate=pl.CostEstimate(flops=0, bytes_accessed=2_000_000, transcendentals=0),
        compiler_params=pltpu.CompilerParams(vmem_limit_bytes=60 * 1024 * 1024),
        name="pack_messages",
    )(panel_order, row_block, kernel, samples)
    return messages, picked


def unpack_kernel(order_ref, *refs):
    got, (right_ref, piece_ref, load_ref) = refs[:-3], refs[-3:]
    me = lax.axis_index("cols")
    strata = len(got)
    block_rows = piece_ref.shape[0]
    part_rows = block_rows // strata
    per_place = PANELS * PW * block_rows * lax.axis_size("rows") // (PANELS * PW * PW)
    for k in range(PANELS):
        load_ref[k, block_rows:] = right_ref[k]
        shift = (me - lax.div(order_ref[k], per_place)) & (strata - 1)
        for s in range(strata):

            @pl.when(shift == s)
            def _():
                piece_ref[:, k * PW : (k + 1) * PW] = got[s][:block_rows, k * PW : (k + 1) * PW]
                for row_panel in range(PANELS):
                    lo = block_rows + row_panel * part_rows
                    for chunk in range(k * PW // SIDE, (k + 1) * PW // SIDE):
                        load_ref[row_panel, chunk * part_rows : (chunk + 1) * part_rows] = got[s][
                            lo : lo + part_rows, chunk * SIDE : (chunk + 1) * SIDE
                        ]


def unpack_call(panel_order, got, right):
    block_rows = right.shape[1]
    return pl.pallas_call(
        unpack_kernel,
        in_specs=[pl.BlockSpec(memory_space=pltpu.SMEM)]
        + [pl.BlockSpec(memory_space=pltpu.VMEM)] * (len(got) + 1),
        out_shape=[
            jax.ShapeDtypeStruct((block_rows, PANELS * PW), jnp.float32),
            jax.ShapeDtypeStruct((PANELS, 2 * block_rows, SIDE), jnp.float32),
        ],
        cost_estimate=pl.CostEstimate(flops=0, bytes_accessed=1_000_000, transcendentals=0),
        compiler_params=pltpu.CompilerParams(vmem_limit_bytes=16 * 1024 * 1024),
        name="unpack_messages",
    )(panel_order, *got, right)


def on_device(kernel, row_block, panel_order, samples):
    rows_count, cols_count = lax.axis_size("rows"), lax.axis_size("cols")
    row_place = lax.axis_index("rows")
    block_rows = kernel.shape[0] // row_block.shape[0]
    per_place = kernel.shape[1] // PW

    x_at = [lax.div(lax.rem(panel_order[k], per_place), 4) for k in range(PANELS)]
    z_at = [lax.rem(panel_order[k], 4) for k in range(PANELS)]
    x_here, z_here = row_place >> 4, (row_place >> 2) & 3

    def along_y(array, shift):
        return lax.ppermute(
            array, "cols", [(i, (i + shift) % cols_count) for i in range(cols_count)]
        )

    def along_rows(array, move):
        pairs = []
        for r in range(rows_count):
            x, z, core = move(r // 16, r % 16 // 2, r % 2)
            pairs.append((r, x % 4 * 16 + z % 8 * 2 + core))
        return lax.ppermute(array, "rows", pairs)

    def along_x(array, shift):
        return along_rows(array, lambda x, z, c: (x + shift, z, c))

    def along_z(array, shift):
        return along_rows(array, lambda x, z, c: (x, z + shift, c))

    def to_core(array):
        return along_rows(array, lambda x, z, c: (x, z, c ^ 1))

    def other_half(array, other, swap):
        return jnp.stack([jnp.where(swap[k], other[k], array[k]) for k in range(PANELS)])

    def choose(array, move, at, here):
        other = along_rows(array, move[0])
        array = other_half(array, other, [at[k] == (here ^ 1) for k in range(PANELS)])
        other = along_rows(array, move[1])
        return other_half(array, other, [(at[k] >> 1) != (here >> 1) for k in range(PANELS)])

    messages, right = pack_call(panel_order, row_block, kernel, samples)
    got = messages[:1] + [along_y(messages[s], s) for s in range(1, cols_count)]
    piece, load = unpack_call(panel_order, got, right)

    sides = [along_x(piece, s) for s in range(1, 4)]
    pieces = [piece] + [along_y(piece, s) for s in range(1, cols_count)]
    z_moves = (
        lambda x, z, c: (x, (z // 2 ^ 1) * 2 + z % 2, c),
        lambda x, z, c: (x, (3 - z // 2) * 2 + z % 2, c),
    )
    load = choose(load, z_moves, z_at, z_here)
    load, *pieces = lax.optimization_barrier((load, *pieces))
    ring = jnp.concatenate([piece] + sides, 0)
    up, down = along_z(ring, 1), along_z(ring, -1)
    arrays, moves = [ring, up, down], [(0, 0), (1, 0), (-1, 0)]

    x_moves = (lambda x, z, c: (x ^ 1, z, c), lambda x, z, c: (3 - x, z, c))
    load = choose(load, x_moves, x_at, x_here)
    load, up, down = lax.optimization_barrier((load, up, down))
    other = along_rows(load, lambda x, z, c: (x, z ^ 1, c))
    load = jnp.stack([load, other])
    up, down = along_z(up, 1), along_z(down, -1)
    arrays, moves = arrays + [up, down], moves + [(2, 0), (-2, 0)]
    shares, right = load[:, :, :block_rows], load[:, :, block_rows:]
    load = jnp.stack([shares] + [along_y(shares, s) for s in range(1, cols_count)] + [right])
    load, up, down = lax.optimization_barrier((load, up, down))
    other = to_core(load)
    up, down = along_z(up, 1), along_z(down, -1)
    arrays, moves = arrays + [up, down], moves + [(3, 0), (-3, 0)]

    v1, rest, under, right = first_call(load, other)
    rest, under, *arrays = lax.optimization_barrier((rest, under, *arrays))
    up, down = arrays[-2:]
    half = up.shape[0] // 2
    up, down = along_z(up[:half], 1), along_z(down[half:], -1)
    swapped = [to_core(array) for array in arrays]
    v2, cross = second_call(rest, under)
    v2, cross, up, down = lax.optimization_barrier((v2, cross, up, down))
    arrays, moves = arrays + [up, down], moves + [(4, 0), (4, 2)]
    swapped += [to_core(up), to_core(down)]
    factor, weights, solved, reduced = apply_call(row_block, pieces, v1, cross, v2, right, samples)
    moves = [(dz, first, c) for c in range(2) for dz, first in moves]
    trailing = update_call(kernel, weights, arrays + swapped, moves)
    return trailing, factor, solved, reduced


def solution(mesh):
    in_specs = (P("rows", "cols"), P("rows"), P(), P("rows", "cols"))
    out_specs = (P("rows", "cols"), P("rows", None), P(None, "cols"), P("rows", "cols"))
    return jax.shard_map(
        on_device, mesh=mesh, in_specs=in_specs, out_specs=out_specs, check_vma=False
    )
```

```python
import jax
import jax.numpy as jnp
from jax import lax
from jax.experimental import pallas as pl
from jax.experimental.pallas import tpu as pltpu
from jax.sharding import PartitionSpec as P

PW = 256
PANELS = 2
EXACT = lax.Precision.HIGHEST
SIDE = 128
STEP = 8


def dot_nt(a, b, precision=EXACT):
    return lax.dot_general(a, b, (((1,), (1,)), ((), ())), precision=precision, preferred_element_type=jnp.float32)


def dot_nn(a, b, precision=EXACT):
    return lax.dot_general(a, b, (((1,), (0,)), ((), ())), precision=precision, preferred_element_type=jnp.float32)


def lanes_of(rows, lane):
    return jnp.broadcast_to(rows[:, lane : lane + 1], (STEP, SIDE))


def sublanes_of(rows, sub):
    return jnp.broadcast_to(rows[sub : sub + 1, :], (STEP, SIDE))


def small_inverse(spread):
    inv, low = [None] * STEP, [[None] * STEP for _ in range(STEP)]
    rest = [list(r) for r in spread]
    for s in range(STEP):
        inv[s] = lax.rsqrt(rest[s][s])
        for r in range(s + 1, STEP):
            low[r][s] = rest[r][s] * inv[s]
        for r in range(s + 1, STEP):
            for q in range(s + 1, r + 1):
                rest[r][q] = rest[r][q] - low[r][s] * low[q][s]
    out = [[None] * STEP for _ in range(STEP)]
    for r in range(STEP):
        out[r][r] = inv[r]
        for s in range(r):
            total = low[r][s] * out[s][s]
            for q in range(s + 1, r):
                total = total + low[r][q] * out[q][s]
            out[r][s] = -inv[r] * total
    return out


def tile_inverse(d_ref, x_ref):
    groups = SIDE // STEP
    sub = lax.broadcasted_iota(jnp.int32, (STEP, SIDE), 0)
    lane = lax.broadcasted_iota(jnp.int32, (STEP, SIDE), 1)
    left = [d_ref[STEP * g : STEP * (g + 1), :] for g in range(groups)]
    right = [jnp.where(lane == sub + STEP * g, 1.0, 0.0).astype(jnp.float32) for g in range(groups)]
    for b in range(groups):
        here_l, here_r = left[b], right[b]
        cols = [lanes_of(here_l, STEP * b + s) for s in range(STEP)]
        spread = [[sublanes_of(cols[s], r) if s <= r else None for s in range(STEP)] for r in range(STEP)]
        v = small_inverse(spread)
        in_l = [sublanes_of(here_l, s) for s in range(STEP)]
        in_r = [sublanes_of(here_r, s) for s in range(STEP)]
        out_l, out_r = [], []
        for r in range(STEP):
            tl, tr = v[r][0] * in_l[0], v[r][0] * in_r[0]
            for s in range(1, r + 1):
                tl, tr = tl + v[r][s] * in_l[s], tr + v[r][s] * in_r[s]
            out_l.append(tl)
            out_r.append(tr)
        new_r = out_r[0]
        for r in range(1, STEP):
            new_r = jnp.where(sub == r, out_r[r], new_r)
        x_ref[STEP * b : STEP * (b + 1), :] = new_r
        if b + 1 == groups:
            break
        t_l, t_r = [], []
        for s in range(STEP):
            tl, tr = v[STEP - 1][s] * out_l[STEP - 1], v[STEP - 1][s] * out_r[STEP - 1]
            for r in range(s, STEP - 1):
                tl, tr = tl + v[r][s] * out_l[r], tr + v[r][s] * out_r[r]
            t_l.append(tl)
            t_r.append(tr)
        for g in range(b + 1, groups):
            c = [lanes_of(left[g], STEP * b + s) for s in range(STEP)]
            sl, sr = c[0] * t_l[0], c[0] * t_r[0]
            for s in range(1, STEP):
                sl, sr = sl + c[s] * t_l[s], sr + c[s] * t_r[s]
            left[g], right[g] = left[g] - sl, right[g] - sr


def halves(array):
    high = array.astype(jnp.bfloat16)
    return high, (array - high.astype(jnp.float32)).astype(jnp.bfloat16)


def two_tiles(a, v, d, x):
    v[...] = jnp.zeros_like(v)

    @pl.loop(0, 2)
    def _(k):
        at = pl.multiple_of(k * SIDE, SIDE)
        d[...] = a[pl.ds(at, SIDE), pl.ds(at, SIDE)]
        tile_inverse(d, x)

        @pl.when(k == 0)
        def _():
            own = x[...]
            v[:SIDE, :SIDE] = own
            below = dot_nt(a[SIDE:, :SIDE], own)
            a[SIDE:, SIDE:] = a[SIDE:, SIDE:] - dot_nt(below, below)
            v[SIDE:, :SIDE] = -dot_nn(below, own)

        @pl.when(k == 1)
        def _():
            own = x[...]
            v[SIDE:, SIDE:] = own
            v[SIDE:, :SIDE] = dot_nn(own, v[SIDE:, :SIDE])


def first_kernel(own_ref, other_ref, v_ref, rest_ref, under_ref, right_ref, a, top, d, x):
    row_place, col_place = lax.axis_index("rows"), lax.axis_index("cols")
    core, odd = row_place & 1, (row_place >> 1) & 1
    strata = lax.axis_size("cols")
    share = own_ref.shape[0] // (strata + 1)
    part_rows = share // (2 * PANELS)
    block_rows = part_rows * strata
    for c, source in enumerate((own_ref, other_ref)):
        for z in range(2):
            member = (odd ^ z) * 2 + (core ^ c)
            for k in range(PANELS):
                base = k * PW + member * block_rows
                lo = (z * PANELS + k) * part_rows
                for shift in range(strata):
                    part = (col_place - shift) & (strata - 1)
                    at = pl.multiple_of(base + part * part_rows, part_rows)
                    a[pl.ds(at, part_rows), :] = source[shift * share + lo : shift * share + lo + part_rows, :]
                for chunk in range(block_rows // part_rows):
                    at = pl.multiple_of(base + chunk * part_rows, part_rows)
                    right_ref[pl.ds(at, part_rows), :] = source[
                        strata * share + lo : strata * share + lo + part_rows, chunk * SIDE : (chunk + 1) * SIDE
                    ]
    top[...] = a[:PW, :PW]
    two_tiles(top, v_ref, d, x)
    v = v_ref[...]
    low = dot_nt(a[PW:, :PW], v)
    rest_ref[...] = a[PW:, PW:] - dot_nt(low, low)
    under_ref[...] = -dot_nn(low, v)


def square(side):
    return jax.ShapeDtypeStruct((side, side), jnp.float32)


def first_call(own, other):
    right = jax.ShapeDtypeStruct((PANELS * PW, SIDE), jnp.float32)
    return pl.pallas_call(
        first_kernel,
        out_shape=[square(PW), square(PW), square(PW), right],
        scratch_shapes=[
            pltpu.VMEM((PANELS * PW, PANELS * PW), jnp.float32),
            pltpu.VMEM((PW, PW), jnp.float32),
            pltpu.VMEM((SIDE, SIDE), jnp.float32),
            pltpu.VMEM((SIDE, SIDE), jnp.float32),
        ],
        cost_estimate=pl.CostEstimate(flops=12_000_000_000, bytes_accessed=2_000_000, transcendentals=0),
        compiler_params=pltpu.CompilerParams(vmem_limit_bytes=16 * 1024 * 1024),
        name="eliminate_first",
    )(own, other)


def second_kernel(rest_ref, under_ref, v_ref, cross_ref, a, d, x):
    a[...] = rest_ref[...]
    two_tiles(a, v_ref, d, x)
    cross_ref[...] = dot_nn(v_ref[...], under_ref[...])


def second_call(rest, under):
    return pl.pallas_call(
        second_kernel,
        out_shape=[square(PW), square(PW)],
        scratch_shapes=[
            pltpu.VMEM((PW, PW), jnp.float32),
            pltpu.VMEM((SIDE, SIDE), jnp.float32),
            pltpu.VMEM((SIDE, SIDE), jnp.float32),
        ],
        cost_estimate=pl.CostEstimate(flops=12_000_000_000, bytes_accessed=2_000_000, transcendentals=0),
        compiler_params=pltpu.CompilerParams(vmem_limit_bytes=16 * 1024 * 1024),
        name="eliminate_second",
    )(rest, under)


def apply_kernel(block_ref, *refs):
    pieces, (v1_ref, cross_ref, v2_ref, rc_ref, ri_ref, f_ref, w_ref, y_ref, r_ref, p) = refs[:-10], refs[-10:]
    me = lax.axis_index("cols")
    rows_count = lax.axis_size("rows")
    block_rows = pieces[0].shape[0]
    for u in range(len(pieces)):
        shift = (me - lax.div(block_ref[u], rows_count)) & (len(pieces) - 1)
        for s, piece in enumerate(pieces):

            @pl.when(shift == s)
            def _():
                p[u * block_rows : (u + 1) * block_rows] = piece[...]

    v1, cross, v2 = v1_ref[...], cross_ref[...], v2_ref[...]
    p1, p2 = p[:, :PW], p[:, PW:]
    f1 = dot_nt(p1, v1)
    f2 = dot_nt(p1, cross) + dot_nt(p2, v2)
    f_ref[:, :PW] = f1
    f_ref[:, PW:] = f2
    w_ref[:, :PW] = dot_nn(f1, v1) + dot_nn(f2, cross)
    w_ref[:, PW:] = dot_nn(f2, v2)
    y1 = dot_nn(v1, rc_ref[:PW])
    y2 = dot_nn(cross, rc_ref[:PW]) + dot_nn(v2, rc_ref[PW:])
    y_ref[:PW] = y1
    y_ref[PW:] = y2
    r_ref[...] = ri_ref[...] - dot_nn(f1, y1) - dot_nn(f2, y2)


def apply_call(row_block, pieces, v1, cross, v2, rc, ri):
    size, right = rc.shape
    rows = ri.shape[0]
    f32 = jnp.float32
    operands = (*pieces, v1, cross, v2, rc, ri)
    return pl.pallas_call(
        apply_kernel,
        in_specs=[pl.BlockSpec(memory_space=pltpu.SMEM)]
        + [pl.BlockSpec(memory_space=pltpu.VMEM)] * len(operands),
        out_shape=[
            jax.ShapeDtypeStruct((rows, size), f32),
            jax.ShapeDtypeStruct((rows, size), f32),
            jax.ShapeDtypeStruct((size, right), f32),
            jax.ShapeDtypeStruct((rows, right), f32),
        ],
        scratch_shapes=[pltpu.VMEM((rows, size), f32)],
        cost_estimate=pl.CostEstimate(flops=4_000_000_000, bytes_accessed=4_000_000, transcendentals=0),
        compiler_params=pltpu.CompilerParams(vmem_limit_bytes=16 * 1024 * 1024),
        name="apply_factor",
    )(row_block, *operands)


WIDTH = 512


def update_kernel(moves, k_ref, w_ref, *refs):
    arrays, (o_ref, held, high, low, out, in_sems, out_sems) = refs[:-7], refs[-7:]
    cols = k_ref.shape[1]
    count = cols // WIDTH
    loads = [
        pltpu.make_async_copy(
            k_ref.at[:, i * WIDTH : (i + 1) * WIDTH], held.at[:, i * WIDTH : (i + 1) * WIDTH], in_sems.at[i]
        )
        for i in range(count)
    ]
    for load in loads:
        load.start()
    row_place = lax.axis_index("rows")
    block_rows = cols // lax.axis_size("rows")
    x, z, core = row_place >> 4, (row_place >> 1) & 7, row_place & 1
    for array, (dz, first, swapped) in zip(arrays, moves):
        for part in range(array.shape[0] // block_rows):
            place = ((x - first - part) & 3) * 16 + ((z - dz) & 7) * 2 + (core ^ swapped)
            at = pl.multiple_of(place * block_rows, block_rows)
            top, bottom = halves(array[part * block_rows : (part + 1) * block_rows])
            high[pl.ds(at, block_rows), :] = top
            low[pl.ds(at, block_rows), :] = bottom
    wh, wl = halves(w_ref[...])
    stores = []
    for i in range(count):
        at = slice(i * WIDTH, (i + 1) * WIDTH)
        top, bottom = high[at], low[at]
        total = dot_nt(wh, top, None) + dot_nt(wh, bottom, None) + dot_nt(wl, top, None)
        loads[i].wait()
        out[:, at] = held[:, at] - total
        stores.append(pltpu.make_async_copy(out.at[:, at], o_ref.at[:, at], out_sems.at[i]))
        stores[-1].start()
    for store in stores:
        store.wait()


def update_call(kernel, weights, arrays, moves):
    rows, cols = kernel.shape
    size = weights.shape[1]
    count = cols // WIDTH
    return pl.pallas_call(
        lambda *refs: update_kernel(moves, *refs),
        in_specs=[pl.BlockSpec(memory_space=pltpu.HBM)]
        + [pl.BlockSpec(memory_space=pltpu.VMEM)] * (1 + len(arrays)),
        out_specs=pl.BlockSpec(memory_space=pltpu.HBM),
        out_shape=jax.ShapeDtypeStruct((rows, cols), jnp.float32),
        scratch_shapes=[
            pltpu.VMEM((rows, cols), jnp.float32),
            pltpu.VMEM((cols, size), jnp.bfloat16),
            pltpu.VMEM((cols, size), jnp.bfloat16),
            pltpu.VMEM((rows, cols), jnp.float32),
            pltpu.SemaphoreType.DMA((count,)),
            pltpu.SemaphoreType.DMA((count,)),
        ],
        cost_estimate=pl.CostEstimate(flops=6 * rows * cols * size, bytes_accessed=16_000_000, transcendentals=0),
        compiler_params=pltpu.CompilerParams(vmem_limit_bytes=40 * 1024 * 1024),
        name="trailing_update",
    )(kernel, weights, *arrays)


def pack_kernel(order_ref, block_ref, kernel_ref, samples_ref, *rest):
    messages, right_ref, masks, own, sems = rest[:-5], rest[-5], rest[-4:-2], rest[-2], rest[-1]
    strata = len(messages)
    me = lax.axis_index("cols")
    local_cols = kernel_ref.shape[1]
    blocks_here = strata
    block_rows = kernel_ref.shape[0] // blocks_here
    part_rows = block_rows // strata
    per_place = local_cols // PW
    copies = []
    for k in range(PANELS):
        at = pl.multiple_of(lax.rem(order_ref[k], per_place) * PW, PW)
        copies.append(
            pltpu.make_async_copy(
                kernel_ref.at[:, pl.ds(at, PW)], own.at[:, k * PW : (k + 1) * PW], sems.at[k]
            )
        )
        copies[-1].start()
    rows_count = lax.axis_size("rows")

    def start_of(stratum):
        slot = jnp.int32(0)
        for u in range(blocks_here):
            slot = jnp.where(lax.div(block_ref[u], rows_count) == stratum, u, slot)
        return slot * block_rows

    starts = [start_of(lax.div(order_ref[k], per_place)) for k in range(PANELS)]
    for k in range(PANELS):
        right_ref[k] = samples_ref[pl.ds(pl.multiple_of(starts[k], block_rows), block_rows), :]
    z_here = (lax.axis_index("rows") >> 2) & 3
    for k in range(PANELS):
        z_at = lax.rem(order_ref[k], 4)
        rows = slice(k * 2 * part_rows, (k + 1) * 2 * part_rows)
        swaps = (z_at == (z_here ^ 1), (z_at >> 1) != (z_here >> 1))
        for mask, swap in zip(masks, swaps):
            mask[rows] = jnp.full((2 * part_rows, mask.shape[1]), jnp.where(swap, 1, 0), jnp.int32)
    for copy in copies:
        copy.wait()
    for shift in range(strata):
        to = (me + shift) & (strata - 1)
        out = messages[shift]
        out[:block_rows] = own[pl.ds(pl.multiple_of(start_of(to), block_rows), block_rows), :]
        for k in range(PANELS):
            lo = block_rows + k * part_rows
            at = pl.multiple_of(starts[k] + to * part_rows, part_rows)
            out[lo : lo + part_rows] = own[pl.ds(at, part_rows), :]


def pack_call(panel_order, row_block, kernel, samples):
    strata = lax.axis_size("cols")
    rows, right = samples.shape
    block_rows = rows // row_block.shape[0]
    size = PANELS * PW
    f32 = jnp.float32
    message = pltpu.VMEM((block_rows + PANELS * (block_rows // strata), size), f32)
    mask = pltpu.VMEM((PANELS * 2 * (block_rows // strata), size), jnp.int32)
    *messages, picked, first, second = pl.pallas_call(
        pack_kernel,
        in_specs=[
            pl.BlockSpec(memory_space=pltpu.SMEM),
            pl.BlockSpec(memory_space=pltpu.SMEM),
            pl.BlockSpec(memory_space=pltpu.HBM),
            pl.BlockSpec(memory_space=pltpu.VMEM),
        ],
        out_shape=[message] * strata + [pltpu.VMEM((PANELS, block_rows, right), f32), mask, mask],
        scratch_shapes=[pltpu.VMEM((rows, size), f32), pltpu.SemaphoreType.DMA((PANELS,))],
        cost_estimate=pl.CostEstimate(flops=0, bytes_accessed=2_000_000, transcendentals=0),
        compiler_params=pltpu.CompilerParams(vmem_limit_bytes=60 * 1024 * 1024),
        name="pack_messages",
    )(panel_order, row_block, kernel, samples)
    return messages, picked, (first, second)


def unpack_y_kernel(order_ref, *refs):
    got, (right_ref, out_ref) = refs[:-2], refs[-2:]
    me = lax.axis_index("cols")
    strata = len(got)
    block_rows = right_ref.shape[1]
    part_rows = block_rows // strata
    per_place = block_rows * lax.axis_size("rows") // PW
    for k in range(PANELS):
        columns = slice(k * PW, (k + 1) * PW)
        lo = block_rows + (2 * k + 1) * part_rows
        for chunk in range(strata):
            out_ref[lo : lo + part_rows, chunk * SIDE : (chunk + 1) * SIDE] = right_ref[
                k, chunk * part_rows : (chunk + 1) * part_rows
            ]
        shift = (me - lax.div(order_ref[k], per_place)) & (strata - 1)
        for s in range(strata):

            @pl.when(shift == s)
            def _():
                out_ref[:block_rows, columns] = got[s][:block_rows, columns]
                for row_panel in range(PANELS):
                    source = block_rows + row_panel * part_rows
                    target = block_rows + 2 * row_panel * part_rows
                    out_ref[target : target + part_rows, columns] = got[s][source : source + part_rows, columns]


def unpack_y_call(panel_order, got, right):
    block_rows = right.shape[1]
    strata = len(got)
    rows = block_rows + 2 * PANELS * (block_rows // strata)
    return pl.pallas_call(
        unpack_y_kernel,
        in_specs=[pl.BlockSpec(memory_space=pltpu.SMEM)]
        + [pl.BlockSpec(memory_space=pltpu.VMEM)] * (strata + 1),
        out_shape=jax.ShapeDtypeStruct((rows, PANELS * PW), jnp.float32),
        cost_estimate=pl.CostEstimate(flops=0, bytes_accessed=1_000_000, transcendentals=0),
        compiler_params=pltpu.CompilerParams(vmem_limit_bytes=16 * 1024 * 1024),
        name="unpack_along_y",
    )(panel_order, *got, right)


def unpack_x_kernel(order_ref, *refs):
    got, (ring_ref, load_ref) = refs[:-2], refs[-2:]
    x_here = lax.axis_index("rows") >> 4
    block_rows = ring_ref.shape[0] // len(got)
    rows = load_ref.shape[0] // PANELS
    per_place = block_rows * lax.axis_size("rows") // PW
    for s, source in enumerate(got):
        ring_ref[s * block_rows : (s + 1) * block_rows] = source[:block_rows]
    for k in range(PANELS):
        shift = (x_here - lax.div(lax.rem(order_ref[k], per_place), 4)) & 3
        for s, source in enumerate(got):

            @pl.when(shift == s)
            def _():
                lo = block_rows + k * rows
                load_ref[k * rows : (k + 1) * rows] = source[lo : lo + rows]


def unpack_x_call(panel_order, got, block_rows):
    rows, size = got[0].shape
    f32 = jnp.float32
    return pl.pallas_call(
        unpack_x_kernel,
        in_specs=[pl.BlockSpec(memory_space=pltpu.SMEM)] + [pl.BlockSpec(memory_space=pltpu.VMEM)] * len(got),
        out_shape=[
            jax.ShapeDtypeStruct((len(got) * block_rows, size), f32),
            jax.ShapeDtypeStruct((rows - block_rows, size), f32),
        ],
        cost_estimate=pl.CostEstimate(flops=0, bytes_accessed=1_000_000, transcendentals=0),
        compiler_params=pltpu.CompilerParams(vmem_limit_bytes=16 * 1024 * 1024),
        name="unpack_along_x",
    )(panel_order, *got)


def on_device(kernel, row_block, panel_order, samples):
    rows_count, cols_count = lax.axis_size("rows"), lax.axis_size("cols")
    block_rows = kernel.shape[0] // row_block.shape[0]
    part_rows = block_rows // cols_count

    def along_y(array, shift):
        return lax.ppermute(
            array, "cols", [(i, (i + shift) % cols_count) for i in range(cols_count)]
        )

    def along_rows(array, move):
        pairs = []
        for r in range(rows_count):
            x, z, core = move(r // 16, r % 16 // 2, r % 2)
            pairs.append((r, x % 4 * 16 + z % 8 * 2 + core))
        return lax.ppermute(array, "rows", pairs)

    def along_x(array, shift):
        return along_rows(array, lambda x, z, c: (x + shift, z, c))

    def along_z(array, shift):
        return along_rows(array, lambda x, z, c: (x, z + shift, c))

    def to_core(array):
        return along_rows(array, lambda x, z, c: (x, z, c ^ 1))

    messages, right, masks = pack_call(panel_order, row_block, kernel, samples)
    got = messages[:1] + [along_y(messages[s], s) for s in range(1, cols_count)]
    message = unpack_y_call(panel_order, got, right)
    piece = message[:block_rows]

    got = [message] + [along_x(message, s) for s in range(1, 4)]
    pieces = [piece] + [along_y(piece, s) for s in range(1, cols_count)]
    ring, load = unpack_x_call(panel_order, got, block_rows)
    ring, load, *pieces = lax.optimization_barrier((ring, load, *pieces))

    other = along_rows(load, lambda x, z, c: (x, (z // 2 ^ 1) * 2 + z % 2, c))
    load = jnp.where(masks[0] != 0, other, load)
    up, down = along_z(ring, 1), along_z(ring, -1)
    arrays, moves = [ring, up, down], [(0, 0), (1, 0), (-1, 0)]
    other = along_rows(load, lambda x, z, c: (x, (3 - z // 2) * 2 + z % 2, c))
    load = jnp.where(masks[1] != 0, other, load)
    other = along_rows(load, lambda x, z, c: (x, z ^ 1, c))
    load, other, up, down = lax.optimization_barrier((load, other, up, down))
    up, down = along_z(up, 1), along_z(down, -1)
    arrays, moves = arrays + [up, down], moves + [(2, 0), (-2, 0)]

    def part(array, first):
        at = [(2 * k + first) * part_rows for k in range(PANELS)]
        return [array[lo : lo + part_rows] for lo in at]

    shares = jnp.concatenate(part(load, 0) + part(other, 0), 0)
    rights = jnp.concatenate(part(load, 1) + part(other, 1), 0)
    load = jnp.concatenate([shares] + [along_y(shares, s) for s in range(1, cols_count)] + [rights], 0)
    load, up, down = lax.optimization_barrier((load, up, down))
    other = to_core(load)
    up, down = along_z(up, 1), along_z(down, -1)
    arrays, moves = arrays + [up, down], moves + [(3, 0), (-3, 0)]

    v1, rest, under, right = first_call(load, other)
    rest, under, *arrays = lax.optimization_barrier((rest, under, *arrays))
    up, down = arrays[-2:]
    half = up.shape[0] // 2
    up, down = along_z(up[:half], 1), along_z(down[half:], -1)
    swapped = [to_core(array) for array in arrays]
    v2, cross = second_call(rest, under)
    v2, cross, up, down = lax.optimization_barrier((v2, cross, up, down))
    arrays, moves = arrays + [up, down], moves + [(4, 0), (4, 2)]
    swapped += [to_core(up), to_core(down)]
    factor, weights, solved, reduced = apply_call(row_block, pieces, v1, cross, v2, right, samples)
    moves = [(dz, first, c) for c in range(2) for dz, first in moves]
    trailing = update_call(kernel, weights, arrays + swapped, moves)
    return trailing, factor, solved, reduced


def solution(mesh):
    in_specs = (P("rows", "cols"), P("rows"), P(), P("rows", "cols"))
    out_specs = (P("rows", "cols"), P("rows", None), P(None, "cols"), P("rows", "cols"))
    return jax.shard_map(
        on_device, mesh=mesh, in_specs=in_specs, out_specs=out_specs, check_vma=False
    )
```

```python
import jax
import jax.numpy as jnp
from jax import lax
from jax.experimental import pallas as pl
from jax.experimental.pallas import tpu as pltpu
from jax.sharding import PartitionSpec as P

PW = 256
PANELS = 2
EXACT = lax.Precision.HIGHEST
SIDE = 128
STEP = 8


def dot_nt(a, b, precision=EXACT):
    return lax.dot_general(a, b, (((1,), (1,)), ((), ())), precision=precision, preferred_element_type=jnp.float32)


def dot_nn(a, b, precision=EXACT):
    return lax.dot_general(a, b, (((1,), (0,)), ((), ())), precision=precision, preferred_element_type=jnp.float32)


def lanes_of(rows, lane):
    return jnp.broadcast_to(rows[:, lane : lane + 1], (STEP, SIDE))


def sublanes_of(rows, sub):
    return jnp.broadcast_to(rows[sub : sub + 1, :], (STEP, SIDE))


def small_inverse(spread):
    inv, low = [None] * STEP, [[None] * STEP for _ in range(STEP)]
    rest = [list(r) for r in spread]
    for s in range(STEP):
        inv[s] = lax.rsqrt(rest[s][s])
        for r in range(s + 1, STEP):
            low[r][s] = rest[r][s] * inv[s]
        for r in range(s + 1, STEP):
            for q in range(s + 1, r + 1):
                rest[r][q] = rest[r][q] - low[r][s] * low[q][s]
    out = [[None] * STEP for _ in range(STEP)]
    for r in range(STEP):
        out[r][r] = inv[r]
        for s in range(r):
            total = low[r][s] * out[s][s]
            for q in range(s + 1, r):
                total = total + low[r][q] * out[q][s]
            out[r][s] = -inv[r] * total
    return out


def tile_inverse(d_ref, x_ref):
    groups = SIDE // STEP
    sub = lax.broadcasted_iota(jnp.int32, (STEP, SIDE), 0)
    lane = lax.broadcasted_iota(jnp.int32, (STEP, SIDE), 1)
    left = [d_ref[STEP * g : STEP * (g + 1), :] for g in range(groups)]
    right = [jnp.where(lane == sub + STEP * g, 1.0, 0.0).astype(jnp.float32) for g in range(groups)]
    for b in range(groups):
        here_l, here_r = left[b], right[b]
        cols = [lanes_of(here_l, STEP * b + s) for s in range(STEP)]
        spread = [[sublanes_of(cols[s], r) if s <= r else None for s in range(STEP)] for r in range(STEP)]
        v = small_inverse(spread)
        in_l = [sublanes_of(here_l, s) for s in range(STEP)]
        in_r = [sublanes_of(here_r, s) for s in range(STEP)]
        out_l, out_r = [], []
        for r in range(STEP):
            tl, tr = v[r][0] * in_l[0], v[r][0] * in_r[0]
            for s in range(1, r + 1):
                tl, tr = tl + v[r][s] * in_l[s], tr + v[r][s] * in_r[s]
            out_l.append(tl)
            out_r.append(tr)
        new_r = out_r[0]
        for r in range(1, STEP):
            new_r = jnp.where(sub == r, out_r[r], new_r)
        x_ref[STEP * b : STEP * (b + 1), :] = new_r
        if b + 1 == groups:
            break
        t_l, t_r = [], []
        for s in range(STEP):
            tl, tr = v[STEP - 1][s] * out_l[STEP - 1], v[STEP - 1][s] * out_r[STEP - 1]
            for r in range(s, STEP - 1):
                tl, tr = tl + v[r][s] * out_l[r], tr + v[r][s] * out_r[r]
            t_l.append(tl)
            t_r.append(tr)
        for g in range(b + 1, groups):
            c = [lanes_of(left[g], STEP * b + s) for s in range(STEP)]
            sl, sr = c[0] * t_l[0], c[0] * t_r[0]
            for s in range(1, STEP):
                sl, sr = sl + c[s] * t_l[s], sr + c[s] * t_r[s]
            left[g], right[g] = left[g] - sl, right[g] - sr


def halves(array):
    high = array.astype(jnp.bfloat16)
    return high, (array - high.astype(jnp.float32)).astype(jnp.bfloat16)


def two_tiles(a, v, d, x):
    v[...] = jnp.zeros_like(v)

    @pl.loop(0, 2)
    def _(k):
        at = pl.multiple_of(k * SIDE, SIDE)
        d[...] = a[pl.ds(at, SIDE), pl.ds(at, SIDE)]
        tile_inverse(d, x)

        @pl.when(k == 0)
        def _():
            own = x[...]
            v[:SIDE, :SIDE] = own
            below = dot_nt(a[SIDE:, :SIDE], own)
            a[SIDE:, SIDE:] = a[SIDE:, SIDE:] - dot_nt(below, below)
            v[SIDE:, :SIDE] = -dot_nn(below, own)

        @pl.when(k == 1)
        def _():
            own = x[...]
            v[SIDE:, SIDE:] = own
            v[SIDE:, :SIDE] = dot_nn(own, v[SIDE:, :SIDE])


def first_kernel(own_ref, other_ref, v_ref, rest_ref, under_ref, right_ref, a, top, d, x):
    row_place, col_place = lax.axis_index("rows"), lax.axis_index("cols")
    core, odd = row_place & 1, (row_place >> 1) & 1
    strata = lax.axis_size("cols")
    share = own_ref.shape[0] // (strata + 1)
    part_rows = share // (2 * PANELS)
    block_rows = part_rows * strata
    for c, source in enumerate((own_ref, other_ref)):
        for z in range(2):
            member = (odd ^ z) * 2 + (core ^ c)
            for k in range(PANELS):
                base = k * PW + member * block_rows
                lo = (z * PANELS + k) * part_rows
                for shift in range(strata):
                    part = (col_place - shift) & (strata - 1)
                    at = pl.multiple_of(base + part * part_rows, part_rows)
                    a[pl.ds(at, part_rows), :] = source[shift * share + lo : shift * share + lo + part_rows, :]
                for chunk in range(block_rows // part_rows):
                    at = pl.multiple_of(base + chunk * part_rows, part_rows)
                    right_ref[pl.ds(at, part_rows), :] = source[
                        strata * share + lo : strata * share + lo + part_rows, chunk * SIDE : (chunk + 1) * SIDE
                    ]
    top[...] = a[:PW, :PW]
    two_tiles(top, v_ref, d, x)
    v = v_ref[...]
    low = dot_nt(a[PW:, :PW], v)
    rest_ref[...] = a[PW:, PW:] - dot_nt(low, low)
    under_ref[...] = -dot_nn(low, v)


def square(side):
    return jax.ShapeDtypeStruct((side, side), jnp.float32)


def first_call(own, other):
    right = jax.ShapeDtypeStruct((PANELS * PW, SIDE), jnp.float32)
    return pl.pallas_call(
        first_kernel,
        out_shape=[square(PW), square(PW), square(PW), right],
        scratch_shapes=[
            pltpu.VMEM((PANELS * PW, PANELS * PW), jnp.float32),
            pltpu.VMEM((PW, PW), jnp.float32),
            pltpu.VMEM((SIDE, SIDE), jnp.float32),
            pltpu.VMEM((SIDE, SIDE), jnp.float32),
        ],
        cost_estimate=pl.CostEstimate(flops=12_000_000_000, bytes_accessed=2_000_000, transcendentals=0),
        compiler_params=pltpu.CompilerParams(vmem_limit_bytes=16 * 1024 * 1024),
        name="eliminate_first",
    )(own, other)


def second_kernel(rest_ref, under_ref, v_ref, cross_ref, a, d, x):
    a[...] = rest_ref[...]
    two_tiles(a, v_ref, d, x)
    cross_ref[...] = dot_nn(v_ref[...], under_ref[...])


def second_call(rest, under):
    return pl.pallas_call(
        second_kernel,
        out_shape=[square(PW), square(PW)],
        scratch_shapes=[
            pltpu.VMEM((PW, PW), jnp.float32),
            pltpu.VMEM((SIDE, SIDE), jnp.float32),
            pltpu.VMEM((SIDE, SIDE), jnp.float32),
        ],
        cost_estimate=pl.CostEstimate(flops=12_000_000_000, bytes_accessed=2_000_000, transcendentals=0),
        compiler_params=pltpu.CompilerParams(vmem_limit_bytes=16 * 1024 * 1024),
        name="eliminate_second",
    )(rest, under)


def apply_kernel(block_ref, *refs):
    pieces, (v1_ref, cross_ref, v2_ref, rc_ref, ri_ref, f_ref, w_ref, y_ref, r_ref, p) = refs[:-10], refs[-10:]
    me = lax.axis_index("cols")
    rows_count = lax.axis_size("rows")
    block_rows = pieces[0].shape[0]
    for u in range(len(pieces)):
        shift = (me - lax.div(block_ref[u], rows_count)) & (len(pieces) - 1)
        for s, piece in enumerate(pieces):

            @pl.when(shift == s)
            def _():
                p[u * block_rows : (u + 1) * block_rows] = piece[...]

    v1, cross, v2 = v1_ref[...], cross_ref[...], v2_ref[...]
    p1, p2 = p[:, :PW], p[:, PW:]
    f1 = dot_nt(p1, v1)
    f2 = dot_nt(p1, cross) + dot_nt(p2, v2)
    f_ref[:, :PW] = f1
    f_ref[:, PW:] = f2
    w_ref[:, :PW] = dot_nn(f1, v1) + dot_nn(f2, cross)
    w_ref[:, PW:] = dot_nn(f2, v2)
    y1 = dot_nn(v1, rc_ref[:PW])
    y2 = dot_nn(cross, rc_ref[:PW]) + dot_nn(v2, rc_ref[PW:])
    y_ref[:PW] = y1
    y_ref[PW:] = y2
    r_ref[...] = ri_ref[...] - dot_nn(f1, y1) - dot_nn(f2, y2)


def apply_call(row_block, pieces, v1, cross, v2, rc, ri):
    size, right = rc.shape
    rows = ri.shape[0]
    f32 = jnp.float32
    operands = (*pieces, v1, cross, v2, rc, ri)
    return pl.pallas_call(
        apply_kernel,
        in_specs=[pl.BlockSpec(memory_space=pltpu.SMEM)]
        + [pl.BlockSpec(memory_space=pltpu.VMEM)] * len(operands),
        out_shape=[
            jax.ShapeDtypeStruct((rows, size), f32),
            jax.ShapeDtypeStruct((rows, size), f32),
            jax.ShapeDtypeStruct((size, right), f32),
            jax.ShapeDtypeStruct((rows, right), f32),
        ],
        scratch_shapes=[pltpu.VMEM((rows, size), f32)],
        cost_estimate=pl.CostEstimate(flops=4_000_000_000, bytes_accessed=4_000_000, transcendentals=0),
        compiler_params=pltpu.CompilerParams(vmem_limit_bytes=16 * 1024 * 1024),
        name="apply_factor",
    )(row_block, *operands)


WIDTH = 512


def update_kernel(k_ref, w_ref, b_ref, o_ref, held, gathered, out, k_sems, b_sems, out_sems):
    cols = k_ref.shape[1]
    parts = [slice(i * WIDTH, (i + 1) * WIDTH) for i in range(cols // WIDTH)]
    b_loads = [pltpu.make_async_copy(b_ref.at[at], gathered.at[at], b_sems.at[i]) for i, at in enumerate(parts)]
    k_loads = [pltpu.make_async_copy(k_ref.at[:, at], held.at[:, at], k_sems.at[i]) for i, at in enumerate(parts)]
    for b_load, k_load in zip(b_loads, k_loads):
        b_load.start()
        k_load.start()
    wh, wl = halves(w_ref[...])
    stores = []
    for i, at in enumerate(parts):
        b_loads[i].wait()
        top, bottom = halves(gathered[at])
        total = dot_nt(wh, top, None) + dot_nt(wh, bottom, None) + dot_nt(wl, top, None)
        k_loads[i].wait()
        out[:, at] = held[:, at] - total
        stores.append(pltpu.make_async_copy(out.at[:, at], o_ref.at[:, at], out_sems.at[i]))
        stores[-1].start()
    for store in stores:
        store.wait()


def update_call(kernel, weights, across):
    rows, cols = kernel.shape
    size = weights.shape[1]
    count = cols // WIDTH
    f32 = jnp.float32
    return pl.pallas_call(
        update_kernel,
        in_specs=[
            pl.BlockSpec(memory_space=pltpu.HBM),
            pl.BlockSpec(memory_space=pltpu.VMEM),
            pl.BlockSpec(memory_space=pltpu.HBM),
        ],
        out_specs=pl.BlockSpec(memory_space=pltpu.HBM),
        out_shape=jax.ShapeDtypeStruct((rows, cols), f32),
        scratch_shapes=[
            pltpu.VMEM((rows, cols), f32),
            pltpu.VMEM((cols, size), f32),
            pltpu.VMEM((rows, cols), f32),
            pltpu.SemaphoreType.DMA((count,)),
            pltpu.SemaphoreType.DMA((count,)),
            pltpu.SemaphoreType.DMA((count,)),
        ],
        cost_estimate=pl.CostEstimate(flops=6 * rows * cols * size, bytes_accessed=16_000_000, transcendentals=0),
        compiler_params=pltpu.CompilerParams(vmem_limit_bytes=54 * 1024 * 1024),
        name="trailing_update",
    )(kernel, weights, across)


def pack_kernel(order_ref, block_ref, kernel_ref, samples_ref, *rest):
    messages, right_ref, masks, own, sems = rest[:-5], rest[-5], rest[-4:-2], rest[-2], rest[-1]
    strata = len(messages) // 2
    me = lax.axis_index("cols")
    local_cols = kernel_ref.shape[1]
    blocks_here = strata
    block_rows = kernel_ref.shape[0] // blocks_here
    part_rows = block_rows // strata
    per_place = local_cols // PW
    copies = []
    for k in range(PANELS):
        at = pl.multiple_of(lax.rem(order_ref[k], per_place) * PW, PW)
        copies.append(
            pltpu.make_async_copy(
                kernel_ref.at[:, pl.ds(at, PW)], own.at[:, k * PW : (k + 1) * PW], sems.at[k]
            )
        )
        copies[-1].start()
    rows_count = lax.axis_size("rows")

    def start_of(stratum):
        slot = jnp.int32(0)
        for u in range(blocks_here):
            slot = jnp.where(lax.div(block_ref[u], rows_count) == stratum, u, slot)
        return slot * block_rows

    starts = [start_of(lax.div(order_ref[k], per_place)) for k in range(PANELS)]
    for k in range(PANELS):
        right_ref[k] = samples_ref[pl.ds(pl.multiple_of(starts[k], block_rows), block_rows), :]
    z_here = (lax.axis_index("rows") >> 2) & 3
    for k in range(PANELS):
        z_at = lax.rem(order_ref[k], 4)
        rows = slice(k * 2 * part_rows, (k + 1) * 2 * part_rows)
        swaps = (z_at == (z_here ^ 1), (z_at >> 1) != (z_here >> 1))
        for mask, swap in zip(masks, swaps):
            mask[rows] = jnp.full((2 * part_rows, mask.shape[1]), jnp.where(swap, 1, 0), jnp.int32)
    for copy in copies:
        copy.wait()
    for shift in range(strata):
        to = (me + shift) & (strata - 1)
        out, share = messages[shift], messages[strata + shift]
        out[...] = own[pl.ds(pl.multiple_of(start_of(to), block_rows), block_rows), :]
        for k in range(PANELS):
            lo = k * part_rows
            at = pl.multiple_of(starts[k] + to * part_rows, part_rows)
            share[lo : lo + part_rows] = own[pl.ds(at, part_rows), :]


def pack_call(panel_order, row_block, kernel, samples):
    strata = lax.axis_size("cols")
    rows, right = samples.shape
    block_rows = rows // row_block.shape[0]
    size = PANELS * PW
    f32 = jnp.float32
    message = pltpu.VMEM((block_rows, size), f32)
    share = pltpu.VMEM((PANELS * (block_rows // strata), size), f32)
    mask = pltpu.VMEM((PANELS * 2 * (block_rows // strata), size), jnp.int32)
    *messages, picked, first, second = pl.pallas_call(
        pack_kernel,
        in_specs=[
            pl.BlockSpec(memory_space=pltpu.SMEM),
            pl.BlockSpec(memory_space=pltpu.SMEM),
            pl.BlockSpec(memory_space=pltpu.HBM),
            pl.BlockSpec(memory_space=pltpu.VMEM),
        ],
        out_shape=[message] * strata
        + [share] * strata
        + [pltpu.VMEM((PANELS, block_rows, right), f32), mask, mask],
        scratch_shapes=[pltpu.VMEM((rows, size), f32), pltpu.SemaphoreType.DMA((PANELS,))],
        cost_estimate=pl.CostEstimate(flops=0, bytes_accessed=2_000_000, transcendentals=0),
        compiler_params=pltpu.CompilerParams(vmem_limit_bytes=60 * 1024 * 1024),
        name="pack_messages",
    )(panel_order, row_block, kernel, samples)
    return messages[:strata], messages[strata:], picked, (first, second)


def shift_of(order_ref, k, axis, strata):
    per_place = lax.axis_size("rows") // strata
    if axis == "cols":
        return (lax.axis_index("cols") - lax.div(order_ref[k], per_place)) & (strata - 1)
    return ((lax.axis_index("rows") >> 4) - lax.div(lax.rem(order_ref[k], per_place), 4)) & 3


def piece_kernel(order_ref, *refs):
    got, out_ref = refs[:-1], refs[-1]
    for k in range(PANELS):
        columns = slice(k * PW, (k + 1) * PW)
        shift = shift_of(order_ref, k, "cols", len(got))
        for s, source in enumerate(got):

            @pl.when(shift == s)
            def _():
                out_ref[:, columns] = source[:, columns]


def share_kernel(order_ref, *refs):
    got, (right_ref, out_ref) = refs[:-2], refs[-2:]
    part_rows = right_ref.shape[1] // len(got)
    for k in range(PANELS):
        columns = slice(k * PW, (k + 1) * PW)
        lo = (2 * k + 1) * part_rows
        for chunk in range(len(got)):
            out_ref[lo : lo + part_rows, chunk * SIDE : (chunk + 1) * SIDE] = right_ref[
                k, chunk * part_rows : (chunk + 1) * part_rows
            ]
        shift = shift_of(order_ref, k, "cols", len(got))
        for s, source in enumerate(got):

            @pl.when(shift == s)
            def _():
                for p in range(PANELS):
                    out_ref[2 * p * part_rows : (2 * p + 1) * part_rows, columns] = source[
                        p * part_rows : (p + 1) * part_rows, columns
                    ]


def load_kernel(order_ref, *refs):
    got, out_ref = refs[:-1], refs[-1]
    rows = out_ref.shape[0] // PANELS
    for k in range(PANELS):
        at = slice(k * rows, (k + 1) * rows)
        shift = shift_of(order_ref, k, "rows", lax.axis_size("cols"))
        for s, source in enumerate(got):

            @pl.when(shift == s)
            def _():
                out_ref[at] = source[at]


def choose_call(body, panel_order, got, rows, name):
    return pl.pallas_call(
        body,
        in_specs=[pl.BlockSpec(memory_space=pltpu.SMEM)] + [pl.BlockSpec(memory_space=pltpu.VMEM)] * len(got),
        out_shape=jax.ShapeDtypeStruct((rows, PANELS * PW), jnp.float32),
        cost_estimate=pl.CostEstimate(flops=0, bytes_accessed=1_000_000, transcendentals=0),
        compiler_params=pltpu.CompilerParams(vmem_limit_bytes=16 * 1024 * 1024),
        name=name,
    )(panel_order, *got)


def on_device(kernel, row_block, panel_order, samples):
    rows_count, cols_count = lax.axis_size("rows"), lax.axis_size("cols")
    block_rows = kernel.shape[0] // row_block.shape[0]
    part_rows = block_rows // cols_count

    def along_y(array, shift):
        return lax.ppermute(
            array, "cols", [(i, (i + shift) % cols_count) for i in range(cols_count)]
        )

    def along_rows(array, move):
        pairs = []
        for r in range(rows_count):
            x, z, core = move(r // 16, r % 16 // 2, r % 2)
            pairs.append((r, x % 4 * 16 + z % 8 * 2 + core))
        return lax.ppermute(array, "rows", pairs)

    def along_x(array, shift):
        return along_rows(array, lambda x, z, c: (x + shift, z, c))

    def to_core(array):
        return along_rows(array, lambda x, z, c: (x, z, c ^ 1))

    messages, shares, right, masks = pack_call(panel_order, row_block, kernel, samples)
    got = messages[:1] + [along_y(messages[s], s) for s in range(1, cols_count)]
    piece = choose_call(piece_kernel, panel_order, got, block_rows, "choose_pieces")
    across = lax.all_gather(piece, "rows", axis=0, tiled=True)
    got = shares[:1] + [along_y(shares[s], s) for s in range(1, cols_count)]
    load = choose_call(share_kernel, panel_order, [*got, right], block_rows, "choose_shares")

    got = [load] + [along_x(load, s) for s in range(1, 4)]
    load = choose_call(load_kernel, panel_order, got, block_rows, "choose_along_x")
    pieces = [piece] + [along_y(piece, s) for s in range(1, cols_count)]
    other = along_rows(load, lambda x, z, c: (x, (z // 2 ^ 1) * 2 + z % 2, c))
    load = jnp.where(masks[0] != 0, other, load)
    other = along_rows(load, lambda x, z, c: (x, (3 - z // 2) * 2 + z % 2, c))
    load = jnp.where(masks[1] != 0, other, load)
    load, *pieces = lax.optimization_barrier((load, *pieces))
    other = along_rows(load, lambda x, z, c: (x, z ^ 1, c))

    def part(array, first):
        at = [(2 * k + first) * part_rows for k in range(PANELS)]
        return [array[lo : lo + part_rows] for lo in at]

    shares = jnp.concatenate(part(load, 0) + part(other, 0), 0)
    rights = jnp.concatenate(part(load, 1) + part(other, 1), 0)
    load = jnp.concatenate([shares] + [along_y(shares, s) for s in range(1, cols_count)] + [rights], 0)
    other = to_core(load)

    v1, rest, under, right = first_call(load, other)
    v2, cross = second_call(rest, under)
    factor, weights, solved, reduced = apply_call(row_block, pieces, v1, cross, v2, right, samples)
    trailing = update_call(kernel, weights, across)
    return trailing, factor, solved, reduced


def solution(mesh):
    in_specs = (P("rows", "cols"), P("rows"), P(), P("rows", "cols"))
    out_specs = (P("rows", "cols"), P("rows", None), P(None, "cols"), P("rows", "cols"))
    return jax.shard_map(
        on_device, mesh=mesh, in_specs=in_specs, out_specs=out_specs, check_vma=False
    )
```

```python
import jax
import jax.numpy as jnp
from jax import lax
from jax.experimental import pallas as pl
from jax.experimental.pallas import tpu as pltpu
from jax.sharding import PartitionSpec as P

PW = 256
PANELS = 2
EXACT = lax.Precision.HIGHEST
SIDE = 128
STEP = 8


def dot_nt(a, b, precision=EXACT):
    return lax.dot_general(a, b, (((1,), (1,)), ((), ())), precision=precision, preferred_element_type=jnp.float32)


def dot_nn(a, b, precision=EXACT):
    return lax.dot_general(a, b, (((1,), (0,)), ((), ())), precision=precision, preferred_element_type=jnp.float32)


def lanes_of(rows, lane):
    return jnp.broadcast_to(rows[:, lane : lane + 1], (STEP, SIDE))


def sublanes_of(rows, sub):
    return jnp.broadcast_to(rows[sub : sub + 1, :], (STEP, SIDE))


def small_inverse(spread):
    inv, low = [None] * STEP, [[None] * STEP for _ in range(STEP)]
    rest = [list(r) for r in spread]
    for s in range(STEP):
        inv[s] = lax.rsqrt(rest[s][s])
        for r in range(s + 1, STEP):
            low[r][s] = rest[r][s] * inv[s]
        for r in range(s + 1, STEP):
            for q in range(s + 1, r + 1):
                rest[r][q] = rest[r][q] - low[r][s] * low[q][s]
    out = [[None] * STEP for _ in range(STEP)]
    for r in range(STEP):
        out[r][r] = inv[r]
        for s in range(r):
            total = low[r][s] * out[s][s]
            for q in range(s + 1, r):
                total = total + low[r][q] * out[q][s]
            out[r][s] = -inv[r] * total
    return out


def tile_inverse(d_ref, x_ref):
    groups = SIDE // STEP
    sub = lax.broadcasted_iota(jnp.int32, (STEP, SIDE), 0)
    lane = lax.broadcasted_iota(jnp.int32, (STEP, SIDE), 1)
    left = [d_ref[STEP * g : STEP * (g + 1), :] for g in range(groups)]
    right = [jnp.where(lane == sub + STEP * g, 1.0, 0.0).astype(jnp.float32) for g in range(groups)]
    for b in range(groups):
        here_l, here_r = left[b], right[b]
        cols = [lanes_of(here_l, STEP * b + s) for s in range(STEP)]
        spread = [[sublanes_of(cols[s], r) if s <= r else None for s in range(STEP)] for r in range(STEP)]
        v = small_inverse(spread)
        in_l = [sublanes_of(here_l, s) for s in range(STEP)]
        in_r = [sublanes_of(here_r, s) for s in range(STEP)]
        out_l, out_r = [], []
        for r in range(STEP):
            tl, tr = v[r][0] * in_l[0], v[r][0] * in_r[0]
            for s in range(1, r + 1):
                tl, tr = tl + v[r][s] * in_l[s], tr + v[r][s] * in_r[s]
            out_l.append(tl)
            out_r.append(tr)
        new_r = out_r[0]
        for r in range(1, STEP):
            new_r = jnp.where(sub == r, out_r[r], new_r)
        x_ref[STEP * b : STEP * (b + 1), :] = new_r
        if b + 1 == groups:
            break
        t_l, t_r = [], []
        for s in range(STEP):
            tl, tr = v[STEP - 1][s] * out_l[STEP - 1], v[STEP - 1][s] * out_r[STEP - 1]
            for r in range(s, STEP - 1):
                tl, tr = tl + v[r][s] * out_l[r], tr + v[r][s] * out_r[r]
            t_l.append(tl)
            t_r.append(tr)
        for g in range(b + 1, groups):
            c = [lanes_of(left[g], STEP * b + s) for s in range(STEP)]
            sl, sr = c[0] * t_l[0], c[0] * t_r[0]
            for s in range(1, STEP):
                sl, sr = sl + c[s] * t_l[s], sr + c[s] * t_r[s]
            left[g], right[g] = left[g] - sl, right[g] - sr


def halves(array):
    high = array.astype(jnp.bfloat16)
    return high, (array - high.astype(jnp.float32)).astype(jnp.bfloat16)


def two_tiles(a, v, d, x):
    v[...] = jnp.zeros_like(v)

    @pl.loop(0, 2)
    def _(k):
        at = pl.multiple_of(k * SIDE, SIDE)
        d[...] = a[pl.ds(at, SIDE), pl.ds(at, SIDE)]
        tile_inverse(d, x)

        @pl.when(k == 0)
        def _():
            own = x[...]
            v[:SIDE, :SIDE] = own
            below = dot_nt(a[SIDE:, :SIDE], own)
            a[SIDE:, SIDE:] = a[SIDE:, SIDE:] - dot_nt(below, below)
            v[SIDE:, :SIDE] = -dot_nn(below, own)

        @pl.when(k == 1)
        def _():
            own = x[...]
            v[SIDE:, SIDE:] = own
            v[SIDE:, :SIDE] = dot_nn(own, v[SIDE:, :SIDE])


def first_kernel(own_ref, other_ref, v_ref, rest_ref, under_ref, right_ref, a, top, d, x):
    row_place, col_place = lax.axis_index("rows"), lax.axis_index("cols")
    core, odd = row_place & 1, (row_place >> 1) & 1
    strata = lax.axis_size("cols")
    share = own_ref.shape[0] // (strata + 1)
    part_rows = share // (2 * PANELS)
    block_rows = part_rows * strata
    for c, source in enumerate((own_ref, other_ref)):
        for z in range(2):
            member = (odd ^ z) * 2 + (core ^ c)
            for k in range(PANELS):
                base = k * PW + member * block_rows
                lo = (z * PANELS + k) * part_rows
                for shift in range(strata):
                    part = (col_place - shift) & (strata - 1)
                    at = pl.multiple_of(base + part * part_rows, part_rows)
                    a[pl.ds(at, part_rows), :] = source[shift * share + lo : shift * share + lo + part_rows, :]
                for chunk in range(block_rows // part_rows):
                    at = pl.multiple_of(base + chunk * part_rows, part_rows)
                    right_ref[pl.ds(at, part_rows), :] = source[
                        strata * share + lo : strata * share + lo + part_rows, chunk * SIDE : (chunk + 1) * SIDE
                    ]
    top[...] = a[:PW, :PW]
    two_tiles(top, v_ref, d, x)
    v = v_ref[...]
    low = dot_nt(a[PW:, :PW], v)
    rest_ref[...] = a[PW:, PW:] - dot_nt(low, low)
    under_ref[...] = -dot_nn(low, v)


def square(side):
    return jax.ShapeDtypeStruct((side, side), jnp.float32)


def first_call(own, other):
    right = jax.ShapeDtypeStruct((PANELS * PW, SIDE), jnp.float32)
    return pl.pallas_call(
        first_kernel,
        out_shape=[square(PW), square(PW), square(PW), right],
        scratch_shapes=[
            pltpu.VMEM((PANELS * PW, PANELS * PW), jnp.float32),
            pltpu.VMEM((PW, PW), jnp.float32),
            pltpu.VMEM((SIDE, SIDE), jnp.float32),
            pltpu.VMEM((SIDE, SIDE), jnp.float32),
        ],
        cost_estimate=pl.CostEstimate(flops=12_000_000_000, bytes_accessed=2_000_000, transcendentals=0),
        compiler_params=pltpu.CompilerParams(vmem_limit_bytes=16 * 1024 * 1024),
        name="eliminate_first",
    )(own, other)


def second_kernel(rest_ref, under_ref, v_ref, cross_ref, a, d, x):
    a[...] = rest_ref[...]
    two_tiles(a, v_ref, d, x)
    cross_ref[...] = dot_nn(v_ref[...], under_ref[...])


def second_call(rest, under):
    return pl.pallas_call(
        second_kernel,
        out_shape=[square(PW), square(PW)],
        scratch_shapes=[
            pltpu.VMEM((PW, PW), jnp.float32),
            pltpu.VMEM((SIDE, SIDE), jnp.float32),
            pltpu.VMEM((SIDE, SIDE), jnp.float32),
        ],
        cost_estimate=pl.CostEstimate(flops=12_000_000_000, bytes_accessed=2_000_000, transcendentals=0),
        compiler_params=pltpu.CompilerParams(vmem_limit_bytes=16 * 1024 * 1024),
        name="eliminate_second",
    )(rest, under)


def apply_kernel(block_ref, *refs):
    pieces, (v1_ref, cross_ref, v2_ref, rc_ref, ri_ref, f_ref, w_ref, y_ref, r_ref, p) = refs[:-10], refs[-10:]
    me = lax.axis_index("cols")
    rows_count = lax.axis_size("rows")
    block_rows = pieces[0].shape[0]
    for u in range(len(pieces)):
        shift = (me - lax.div(block_ref[u], rows_count)) & (len(pieces) - 1)
        for s, piece in enumerate(pieces):

            @pl.when(shift == s)
            def _():
                p[u * block_rows : (u + 1) * block_rows] = piece[...]

    v1, cross, v2 = v1_ref[...], cross_ref[...], v2_ref[...]
    p1, p2 = p[:, :PW], p[:, PW:]
    f1 = dot_nt(p1, v1)
    f2 = dot_nt(p1, cross) + dot_nt(p2, v2)
    f_ref[:, :PW] = f1
    f_ref[:, PW:] = f2
    w_ref[:, :PW] = dot_nn(f1, v1) + dot_nn(f2, cross)
    w_ref[:, PW:] = dot_nn(f2, v2)
    y1 = dot_nn(v1, rc_ref[:PW])
    y2 = dot_nn(cross, rc_ref[:PW]) + dot_nn(v2, rc_ref[PW:])
    y_ref[:PW] = y1
    y_ref[PW:] = y2
    r_ref[...] = ri_ref[...] - dot_nn(f1, y1) - dot_nn(f2, y2)


def apply_call(row_block, pieces, v1, cross, v2, rc, ri):
    size, right = rc.shape
    rows = ri.shape[0]
    f32 = jnp.float32
    operands = (*pieces, v1, cross, v2, rc, ri)
    return pl.pallas_call(
        apply_kernel,
        in_specs=[pl.BlockSpec(memory_space=pltpu.SMEM)]
        + [pl.BlockSpec(memory_space=pltpu.VMEM)] * len(operands),
        out_shape=[
            jax.ShapeDtypeStruct((rows, size), f32),
            jax.ShapeDtypeStruct((rows, size), f32),
            jax.ShapeDtypeStruct((size, right), f32),
            jax.ShapeDtypeStruct((rows, right), f32),
        ],
        scratch_shapes=[pltpu.VMEM((rows, size), f32)],
        cost_estimate=pl.CostEstimate(flops=4_000_000_000, bytes_accessed=4_000_000, transcendentals=0),
        compiler_params=pltpu.CompilerParams(vmem_limit_bytes=16 * 1024 * 1024),
        name="apply_factor",
    )(row_block, *operands)


WIDTH = 1024


def update_kernel(k_ref, w_ref, b_ref, o_ref, held, gathered, out, k_sems, b_sems, out_sems):
    cols = k_ref.shape[1]
    parts = [slice(i * WIDTH, (i + 1) * WIDTH) for i in range(cols // WIDTH)]
    b_loads = [pltpu.make_async_copy(b_ref.at[at], gathered.at[at], b_sems.at[i]) for i, at in enumerate(parts)]
    k_loads = [pltpu.make_async_copy(k_ref.at[:, at], held.at[:, at], k_sems.at[i]) for i, at in enumerate(parts)]
    for b_load, k_load in zip(b_loads, k_loads):
        b_load.start()
        k_load.start()
    rows = w_ref.shape[0]
    wh, wl = halves(w_ref[...])
    both = jnp.concatenate([wh, wl], 0)
    stores = []
    for i, at in enumerate(parts):
        b_loads[i].wait()
        top, bottom = halves(gathered[at])
        wide = dot_nt(both, top, None)
        total = wide[:rows] + wide[rows:] + dot_nt(wh, bottom, None)
        k_loads[i].wait()
        out[:, at] = held[:, at] - total
        stores.append(pltpu.make_async_copy(out.at[:, at], o_ref.at[:, at], out_sems.at[i]))
        stores[-1].start()
    for store in stores:
        store.wait()


def update_call(kernel, weights, across):
    rows, cols = kernel.shape
    size = weights.shape[1]
    count = cols // WIDTH
    f32 = jnp.float32
    return pl.pallas_call(
        update_kernel,
        in_specs=[
            pl.BlockSpec(memory_space=pltpu.HBM),
            pl.BlockSpec(memory_space=pltpu.VMEM),
            pl.BlockSpec(memory_space=pltpu.HBM),
        ],
        out_specs=pl.BlockSpec(memory_space=pltpu.HBM),
        out_shape=jax.ShapeDtypeStruct((rows, cols), f32),
        scratch_shapes=[
            pltpu.VMEM((rows, cols), f32),
            pltpu.VMEM((cols, size), f32),
            pltpu.VMEM((rows, cols), f32),
            pltpu.SemaphoreType.DMA((count,)),
            pltpu.SemaphoreType.DMA((count,)),
            pltpu.SemaphoreType.DMA((count,)),
        ],
        cost_estimate=pl.CostEstimate(flops=6 * rows * cols * size, bytes_accessed=16_000_000, transcendentals=0),
        compiler_params=pltpu.CompilerParams(vmem_limit_bytes=54 * 1024 * 1024),
        name="trailing_update",
    )(kernel, weights, across)


def pack_kernel(order_ref, block_ref, kernel_ref, samples_ref, *rest):
    messages, right_ref, masks, own, sems = rest[:-5], rest[-5], rest[-4:-2], rest[-2], rest[-1]
    strata = len(messages) // 2
    me = lax.axis_index("cols")
    local_cols = kernel_ref.shape[1]
    blocks_here = strata
    block_rows = kernel_ref.shape[0] // blocks_here
    part_rows = block_rows // strata
    per_place = local_cols // PW
    copies = []
    for k in range(PANELS):
        at = pl.multiple_of(lax.rem(order_ref[k], per_place) * PW, PW)
        copies.append(
            pltpu.make_async_copy(
                kernel_ref.at[:, pl.ds(at, PW)], own.at[:, k * PW : (k + 1) * PW], sems.at[k]
            )
        )
        copies[-1].start()
    rows_count = lax.axis_size("rows")

    def start_of(stratum):
        slot = jnp.int32(0)
        for u in range(blocks_here):
            slot = jnp.where(lax.div(block_ref[u], rows_count) == stratum, u, slot)
        return slot * block_rows

    starts = [start_of(lax.div(order_ref[k], per_place)) for k in range(PANELS)]
    for k in range(PANELS):
        right_ref[k] = samples_ref[pl.ds(pl.multiple_of(starts[k], block_rows), block_rows), :]
    z_here = (lax.axis_index("rows") >> 2) & 3
    for k in range(PANELS):
        z_at = lax.rem(order_ref[k], 4)
        rows = slice(k * 2 * part_rows, (k + 1) * 2 * part_rows)
        swaps = (z_at == (z_here ^ 1), (z_at >> 1) != (z_here >> 1))
        for mask, swap in zip(masks, swaps):
            mask[rows] = jnp.full((2 * part_rows, mask.shape[1]), jnp.where(swap, 1, 0), jnp.int32)
    for copy in copies:
        copy.wait()
    for shift in range(strata):
        to = (me + shift) & (strata - 1)
        out, share = messages[shift], messages[strata + shift]
        out[...] = own[pl.ds(pl.multiple_of(start_of(to), block_rows), block_rows), :]
        for k in range(PANELS):
            lo = k * part_rows
            at = pl.multiple_of(starts[k] + to * part_rows, part_rows)
            share[lo : lo + part_rows] = own[pl.ds(at, part_rows), :]


def pack_call(panel_order, row_block, kernel, samples):
    strata = lax.axis_size("cols")
    rows, right = samples.shape
    block_rows = rows // row_block.shape[0]
    size = PANELS * PW
    f32 = jnp.float32
    message = pltpu.VMEM((block_rows, size), f32)
    share = pltpu.VMEM((PANELS * (block_rows // strata), size), f32)
    mask = pltpu.VMEM((PANELS * 2 * (block_rows // strata), size), jnp.int32)
    *messages, picked, first, second = pl.pallas_call(
        pack_kernel,
        in_specs=[
            pl.BlockSpec(memory_space=pltpu.SMEM),
            pl.BlockSpec(memory_space=pltpu.SMEM),
            pl.BlockSpec(memory_space=pltpu.HBM),
            pl.BlockSpec(memory_space=pltpu.VMEM),
        ],
        out_shape=[message] * strata
        + [share] * strata
        + [pltpu.VMEM((PANELS, block_rows, right), f32), mask, mask],
        scratch_shapes=[pltpu.VMEM((rows, size), f32), pltpu.SemaphoreType.DMA((PANELS,))],
        cost_estimate=pl.CostEstimate(flops=0, bytes_accessed=2_000_000, transcendentals=0),
        compiler_params=pltpu.CompilerParams(vmem_limit_bytes=60 * 1024 * 1024),
        name="pack_messages",
    )(panel_order, row_block, kernel, samples)
    return messages[:strata], messages[strata:], picked, (first, second)


def shift_of(order_ref, k, axis, strata):
    per_place = lax.axis_size("rows") // strata
    if axis == "cols":
        return (lax.axis_index("cols") - lax.div(order_ref[k], per_place)) & (strata - 1)
    return ((lax.axis_index("rows") >> 4) - lax.div(lax.rem(order_ref[k], per_place), 4)) & 3


def piece_kernel(order_ref, *refs):
    got, out_ref = refs[:-1], refs[-1]
    for k in range(PANELS):
        columns = slice(k * PW, (k + 1) * PW)
        shift = shift_of(order_ref, k, "cols", len(got))
        for s, source in enumerate(got):

            @pl.when(shift == s)
            def _():
                out_ref[:, columns] = source[:, columns]


def share_kernel(order_ref, *refs):
    got, (right_ref, out_ref) = refs[:-2], refs[-2:]
    part_rows = right_ref.shape[1] // len(got)
    for k in range(PANELS):
        columns = slice(k * PW, (k + 1) * PW)
        lo = (2 * k + 1) * part_rows
        for chunk in range(len(got)):
            out_ref[lo : lo + part_rows, chunk * SIDE : (chunk + 1) * SIDE] = right_ref[
                k, chunk * part_rows : (chunk + 1) * part_rows
            ]
        shift = shift_of(order_ref, k, "cols", len(got))
        for s, source in enumerate(got):

            @pl.when(shift == s)
            def _():
                for p in range(PANELS):
                    out_ref[2 * p * part_rows : (2 * p + 1) * part_rows, columns] = source[
                        p * part_rows : (p + 1) * part_rows, columns
                    ]


def load_kernel(order_ref, *refs):
    got, out_ref = refs[:-1], refs[-1]
    rows = out_ref.shape[0] // PANELS
    for k in range(PANELS):
        at = slice(k * rows, (k + 1) * rows)
        shift = shift_of(order_ref, k, "rows", lax.axis_size("cols"))
        for s, source in enumerate(got):

            @pl.when(shift == s)
            def _():
                out_ref[at] = source[at]


def choose_call(body, panel_order, got, rows, name):
    return pl.pallas_call(
        body,
        in_specs=[pl.BlockSpec(memory_space=pltpu.SMEM)] + [pl.BlockSpec(memory_space=pltpu.VMEM)] * len(got),
        out_shape=jax.ShapeDtypeStruct((rows, PANELS * PW), jnp.float32),
        cost_estimate=pl.CostEstimate(flops=0, bytes_accessed=1_000_000, transcendentals=0),
        compiler_params=pltpu.CompilerParams(vmem_limit_bytes=16 * 1024 * 1024),
        name=name,
    )(panel_order, *got)


def on_device(kernel, row_block, panel_order, samples):
    rows_count, cols_count = lax.axis_size("rows"), lax.axis_size("cols")
    block_rows = kernel.shape[0] // row_block.shape[0]
    part_rows = block_rows // cols_count

    def along_y(array, shift):
        return lax.ppermute(
            array, "cols", [(i, (i + shift) % cols_count) for i in range(cols_count)]
        )

    def along_rows(array, move):
        pairs = []
        for r in range(rows_count):
            x, z, core = move(r // 16, r % 16 // 2, r % 2)
            pairs.append((r, x % 4 * 16 + z % 8 * 2 + core))
        return lax.ppermute(array, "rows", pairs)

    def along_x(array, shift):
        return along_rows(array, lambda x, z, c: (x + shift, z, c))

    def to_core(array):
        return along_rows(array, lambda x, z, c: (x, z, c ^ 1))

    messages, shares, right, masks = pack_call(panel_order, row_block, kernel, samples)
    got = messages[:1] + [along_y(messages[s], s) for s in range(1, cols_count)]
    piece = choose_call(piece_kernel, panel_order, got, block_rows, "choose_pieces")
    across = lax.all_gather(piece, "rows", axis=0, tiled=True)
    got = shares[:1] + [along_y(shares[s], s) for s in range(1, cols_count)]
    load = choose_call(share_kernel, panel_order, [*got, right], block_rows, "choose_shares")

    got = [load] + [along_x(load, s) for s in range(1, 4)]
    load = choose_call(load_kernel, panel_order, got, block_rows, "choose_along_x")
    other = along_rows(load, lambda x, z, c: (x, (z // 2 ^ 1) * 2 + z % 2, c))
    load = jnp.where(masks[0] != 0, other, load)
    other = along_rows(load, lambda x, z, c: (x, (3 - z // 2) * 2 + z % 2, c))
    load = jnp.where(masks[1] != 0, other, load)
    other = along_rows(load, lambda x, z, c: (x, z ^ 1, c))

    def part(array, first):
        at = [(2 * k + first) * part_rows for k in range(PANELS)]
        return [array[lo : lo + part_rows] for lo in at]

    shares = jnp.concatenate(part(load, 0) + part(other, 0), 0)
    rights = jnp.concatenate(part(load, 1) + part(other, 1), 0)
    load = jnp.concatenate([shares] + [along_y(shares, s) for s in range(1, cols_count)] + [rights], 0)
    other = to_core(load)
    load, piece = lax.optimization_barrier((load, piece))
    pieces = [piece] + [along_y(piece, s) for s in range(1, cols_count)]

    v1, rest, under, right = first_call(load, other)
    rest, under, *pieces = lax.optimization_barrier((rest, under, *pieces))
    v2, cross = second_call(rest, under)
    factor, weights, solved, reduced = apply_call(row_block, pieces, v1, cross, v2, right, samples)
    trailing = update_call(kernel, weights, across)
    return trailing, factor, solved, reduced


def solution(mesh):
    in_specs = (P("rows", "cols"), P("rows"), P(), P("rows", "cols"))
    out_specs = (P("rows", "cols"), P("rows", None), P(None, "cols"), P("rows", "cols"))
    return jax.shard_map(
        on_device, mesh=mesh, in_specs=in_specs, out_specs=out_specs, check_vma=False
    )
```

```python
import jax
import jax.numpy as jnp
from jax import lax
from jax.experimental import pallas as pl
from jax.experimental.pallas import tpu as pltpu
from jax.sharding import PartitionSpec as P

PW = 256
PANELS = 2
EXACT = lax.Precision.HIGHEST
SIDE = 128
STEP = 8


def dot_nt(a, b, precision=EXACT):
    return lax.dot_general(a, b, (((1,), (1,)), ((), ())), precision=precision, preferred_element_type=jnp.float32)


def dot_nn(a, b, precision=EXACT):
    return lax.dot_general(a, b, (((1,), (0,)), ((), ())), precision=precision, preferred_element_type=jnp.float32)


def lanes_of(rows, lane):
    return jnp.broadcast_to(rows[:, lane : lane + 1], (STEP, SIDE))


def sublanes_of(rows, sub):
    return jnp.broadcast_to(rows[sub : sub + 1, :], (STEP, SIDE))


def small_inverse(spread):
    inv, low = [None] * STEP, [[None] * STEP for _ in range(STEP)]
    rest = [list(r) for r in spread]
    for s in range(STEP):
        inv[s] = lax.rsqrt(rest[s][s])
        for r in range(s + 1, STEP):
            low[r][s] = rest[r][s] * inv[s]
        for r in range(s + 1, STEP):
            for q in range(s + 1, r + 1):
                rest[r][q] = rest[r][q] - low[r][s] * low[q][s]
    out = [[None] * STEP for _ in range(STEP)]
    for r in range(STEP):
        out[r][r] = inv[r]
        for s in range(r):
            total = low[r][s] * out[s][s]
            for q in range(s + 1, r):
                total = total + low[r][q] * out[q][s]
            out[r][s] = -inv[r] * total
    return out


def tile_inverse(d_ref, x_ref):
    groups = SIDE // STEP
    sub = lax.broadcasted_iota(jnp.int32, (STEP, SIDE), 0)
    lane = lax.broadcasted_iota(jnp.int32, (STEP, SIDE), 1)
    left = [d_ref[STEP * g : STEP * (g + 1), :] for g in range(groups)]
    right = [jnp.where(lane == sub + STEP * g, 1.0, 0.0).astype(jnp.float32) for g in range(groups)]
    for b in range(groups):
        here_l, here_r = left[b], right[b]
        cols = [lanes_of(here_l, STEP * b + s) for s in range(STEP)]
        spread = [[sublanes_of(cols[s], r) if s <= r else None for s in range(STEP)] for r in range(STEP)]
        v = small_inverse(spread)
        in_l = [sublanes_of(here_l, s) for s in range(STEP)]
        in_r = [sublanes_of(here_r, s) for s in range(STEP)]
        out_l, out_r = [], []
        for r in range(STEP):
            tl, tr = v[r][0] * in_l[0], v[r][0] * in_r[0]
            for s in range(1, r + 1):
                tl, tr = tl + v[r][s] * in_l[s], tr + v[r][s] * in_r[s]
            out_l.append(tl)
            out_r.append(tr)
        new_r = out_r[0]
        for r in range(1, STEP):
            new_r = jnp.where(sub == r, out_r[r], new_r)
        x_ref[STEP * b : STEP * (b + 1), :] = new_r
        if b + 1 == groups:
            break
        t_l, t_r = [], []
        for s in range(STEP):
            tl, tr = v[STEP - 1][s] * out_l[STEP - 1], v[STEP - 1][s] * out_r[STEP - 1]
            for r in range(s, STEP - 1):
                tl, tr = tl + v[r][s] * out_l[r], tr + v[r][s] * out_r[r]
            t_l.append(tl)
            t_r.append(tr)
        for g in range(b + 1, groups):
            c = [lanes_of(left[g], STEP * b + s) for s in range(STEP)]
            sl, sr = c[0] * t_l[0], c[0] * t_r[0]
            for s in range(1, STEP):
                sl, sr = sl + c[s] * t_l[s], sr + c[s] * t_r[s]
            left[g], right[g] = left[g] - sl, right[g] - sr


def halves(array):
    high = array.astype(jnp.bfloat16)
    return high, (array - high.astype(jnp.float32)).astype(jnp.bfloat16)


def two_tiles(a, v, d, x):
    v[...] = jnp.zeros_like(v)

    @pl.loop(0, 2)
    def _(k):
        at = pl.multiple_of(k * SIDE, SIDE)
        d[...] = a[pl.ds(at, SIDE), pl.ds(at, SIDE)]
        tile_inverse(d, x)

        @pl.when(k == 0)
        def _():
            own = x[...]
            v[:SIDE, :SIDE] = own
            below = dot_nt(a[SIDE:, :SIDE], own)
            a[SIDE:, SIDE:] = a[SIDE:, SIDE:] - dot_nt(below, below)
            v[SIDE:, :SIDE] = -dot_nn(below, own)

        @pl.when(k == 1)
        def _():
            own = x[...]
            v[SIDE:, SIDE:] = own
            v[SIDE:, :SIDE] = dot_nn(own, v[SIDE:, :SIDE])


def first_kernel(own_ref, other_ref, v_ref, rest_ref, under_ref, right_ref, a, top, d, x):
    row_place, col_place = lax.axis_index("rows"), lax.axis_index("cols")
    core, odd = row_place & 1, (row_place >> 1) & 1
    strata = lax.axis_size("cols")
    share = own_ref.shape[0] // (strata + 1)
    part_rows = share // (2 * PANELS)
    block_rows = part_rows * strata
    for c, source in enumerate((own_ref, other_ref)):
        for z in range(2):
            member = (odd ^ z) * 2 + (core ^ c)
            for k in range(PANELS):
                base = k * PW + member * block_rows
                lo = (z * PANELS + k) * part_rows
                for shift in range(strata):
                    part = (col_place - shift) & (strata - 1)
                    at = pl.multiple_of(base + part * part_rows, part_rows)
                    a[pl.ds(at, part_rows), :] = source[shift * share + lo : shift * share + lo + part_rows, :]
                for chunk in range(block_rows // part_rows):
                    at = pl.multiple_of(base + chunk * part_rows, part_rows)
                    right_ref[pl.ds(at, part_rows), :] = source[
                        strata * share + lo : strata * share + lo + part_rows, chunk * SIDE : (chunk + 1) * SIDE
                    ]
    top[...] = a[:PW, :PW]
    two_tiles(top, v_ref, d, x)
    v = v_ref[...]
    low = dot_nt(a[PW:, :PW], v)
    rest_ref[...] = a[PW:, PW:] - dot_nt(low, low)
    under_ref[...] = -dot_nn(low, v)


def square(side):
    return jax.ShapeDtypeStruct((side, side), jnp.float32)


def first_call(own, other):
    right = jax.ShapeDtypeStruct((PANELS * PW, SIDE), jnp.float32)
    return pl.pallas_call(
        first_kernel,
        out_shape=[square(PW), square(PW), square(PW), right],
        scratch_shapes=[
            pltpu.VMEM((PANELS * PW, PANELS * PW), jnp.float32),
            pltpu.VMEM((PW, PW), jnp.float32),
            pltpu.VMEM((SIDE, SIDE), jnp.float32),
            pltpu.VMEM((SIDE, SIDE), jnp.float32),
        ],
        cost_estimate=pl.CostEstimate(flops=12_000_000_000, bytes_accessed=2_000_000, transcendentals=0),
        compiler_params=pltpu.CompilerParams(vmem_limit_bytes=16 * 1024 * 1024),
        name="eliminate_first",
    )(own, other)


def second_kernel(rest_ref, under_ref, v_ref, cross_ref, a, d, x):
    a[...] = rest_ref[...]
    two_tiles(a, v_ref, d, x)
    cross_ref[...] = dot_nn(v_ref[...], under_ref[...])


def second_call(rest, under):
    return pl.pallas_call(
        second_kernel,
        out_shape=[square(PW), square(PW)],
        scratch_shapes=[
            pltpu.VMEM((PW, PW), jnp.float32),
            pltpu.VMEM((SIDE, SIDE), jnp.float32),
            pltpu.VMEM((SIDE, SIDE), jnp.float32),
        ],
        cost_estimate=pl.CostEstimate(flops=12_000_000_000, bytes_accessed=2_000_000, transcendentals=0),
        compiler_params=pltpu.CompilerParams(vmem_limit_bytes=16 * 1024 * 1024),
        name="eliminate_second",
    )(rest, under)


def apply_kernel(block_ref, *refs):
    pieces, (v1_ref, cross_ref, v2_ref, rc_ref, ri_ref, f_ref, w_ref, y_ref, r_ref, p) = refs[:-10], refs[-10:]
    me = lax.axis_index("cols")
    rows_count = lax.axis_size("rows")
    block_rows = pieces[0].shape[0]
    for u in range(len(pieces)):
        shift = (me - lax.div(block_ref[u], rows_count)) & (len(pieces) - 1)
        for s, piece in enumerate(pieces):

            @pl.when(shift == s)
            def _():
                p[u * block_rows : (u + 1) * block_rows] = piece[...]

    v1, cross, v2 = v1_ref[...], cross_ref[...], v2_ref[...]
    p1, p2 = p[:, :PW], p[:, PW:]
    f1 = dot_nt(p1, v1)
    f2 = dot_nt(p1, cross) + dot_nt(p2, v2)
    f_ref[:, :PW] = f1
    f_ref[:, PW:] = f2
    w_ref[:, :PW] = dot_nn(f1, v1) + dot_nn(f2, cross)
    w_ref[:, PW:] = dot_nn(f2, v2)
    y1 = dot_nn(v1, rc_ref[:PW])
    y2 = dot_nn(cross, rc_ref[:PW]) + dot_nn(v2, rc_ref[PW:])
    y_ref[:PW] = y1
    y_ref[PW:] = y2
    r_ref[...] = ri_ref[...] - dot_nn(f1, y1) - dot_nn(f2, y2)


def apply_call(row_block, pieces, v1, cross, v2, rc, ri):
    size, right = rc.shape
    rows = ri.shape[0]
    f32 = jnp.float32
    operands = (*pieces, v1, cross, v2, rc, ri)
    return pl.pallas_call(
        apply_kernel,
        in_specs=[pl.BlockSpec(memory_space=pltpu.SMEM)]
        + [pl.BlockSpec(memory_space=pltpu.VMEM)] * len(operands),
        out_shape=[
            jax.ShapeDtypeStruct((rows, size), f32),
            jax.ShapeDtypeStruct((rows, size), f32),
            jax.ShapeDtypeStruct((size, right), f32),
            jax.ShapeDtypeStruct((rows, right), f32),
        ],
        scratch_shapes=[pltpu.VMEM((rows, size), f32)],
        cost_estimate=pl.CostEstimate(flops=4_000_000_000, bytes_accessed=4_000_000, transcendentals=0),
        compiler_params=pltpu.CompilerParams(vmem_limit_bytes=16 * 1024 * 1024),
        name="apply_factor",
    )(row_block, *operands)


WIDTH = 1024


def update_kernel(k_ref, w_ref, b_ref, o_ref, held, gathered, out, k_sems, b_sems, out_sems):
    cols = k_ref.shape[1]
    parts = [slice(i * WIDTH, (i + 1) * WIDTH) for i in range(cols // WIDTH)]
    b_loads = [pltpu.make_async_copy(b_ref.at[at], gathered.at[at], b_sems.at[i]) for i, at in enumerate(parts)]
    k_loads = [pltpu.make_async_copy(k_ref.at[:, at], held.at[:, at], k_sems.at[i]) for i, at in enumerate(parts)]
    for b_load, k_load in zip(b_loads, k_loads):
        b_load.start()
        k_load.start()
    rows = w_ref.shape[0]
    wh, wl = halves(w_ref[...])
    both = jnp.concatenate([wh, wl], 0)
    stores = []
    for i, at in enumerate(parts):
        b_loads[i].wait()
        top, bottom = halves(gathered[at])
        wide = dot_nt(both, top, None)
        total = wide[:rows] + wide[rows:] + dot_nt(wh, bottom, None)
        k_loads[i].wait()
        out[:, at] = held[:, at] - total
        stores.append(pltpu.make_async_copy(out.at[:, at], o_ref.at[:, at], out_sems.at[i]))
        stores[-1].start()
    for store in stores:
        store.wait()


def update_call(kernel, weights, across):
    rows, cols = kernel.shape
    size = weights.shape[1]
    count = cols // WIDTH
    f32 = jnp.float32
    return pl.pallas_call(
        update_kernel,
        in_specs=[
            pl.BlockSpec(memory_space=pltpu.HBM),
            pl.BlockSpec(memory_space=pltpu.VMEM),
            pl.BlockSpec(memory_space=pltpu.HBM),
        ],
        out_specs=pl.BlockSpec(memory_space=pltpu.HBM),
        out_shape=jax.ShapeDtypeStruct((rows, cols), f32),
        scratch_shapes=[
            pltpu.VMEM((rows, cols), f32),
            pltpu.VMEM((cols, size), f32),
            pltpu.VMEM((rows, cols), f32),
            pltpu.SemaphoreType.DMA((count,)),
            pltpu.SemaphoreType.DMA((count,)),
            pltpu.SemaphoreType.DMA((count,)),
        ],
        cost_estimate=pl.CostEstimate(flops=6 * rows * cols * size, bytes_accessed=16_000_000, transcendentals=0),
        compiler_params=pltpu.CompilerParams(vmem_limit_bytes=50 * 1024 * 1024),
        name="trailing_update",
    )(kernel, weights, across)


def pack_kernel(order_ref, block_ref, kernel_ref, samples_ref, *rest):
    messages, right_ref, masks, own, sems = rest[:-5], rest[-5], rest[-4:-2], rest[-2], rest[-1]
    strata = len(messages) // 2
    me = lax.axis_index("cols")
    local_cols = kernel_ref.shape[1]
    blocks_here = strata
    block_rows = kernel_ref.shape[0] // blocks_here
    part_rows = block_rows // strata
    per_place = local_cols // PW
    copies = []
    for k in range(PANELS):
        at = pl.multiple_of(lax.rem(order_ref[k], per_place) * PW, PW)
        copies.append(
            pltpu.make_async_copy(
                kernel_ref.at[:, pl.ds(at, PW)], own.at[:, k * PW : (k + 1) * PW], sems.at[k]
            )
        )
        copies[-1].start()
    rows_count = lax.axis_size("rows")

    def start_of(stratum):
        slot = jnp.int32(0)
        for u in range(blocks_here):
            slot = jnp.where(lax.div(block_ref[u], rows_count) == stratum, u, slot)
        return slot * block_rows

    starts = [start_of(lax.div(order_ref[k], per_place)) for k in range(PANELS)]
    for k in range(PANELS):
        right_ref[k] = samples_ref[pl.ds(pl.multiple_of(starts[k], block_rows), block_rows), :]
    z_here = (lax.axis_index("rows") >> 2) & 3
    for k in range(PANELS):
        z_at = lax.rem(order_ref[k], 4)
        rows = slice(k * 2 * part_rows, (k + 1) * 2 * part_rows)
        swaps = (z_at == (z_here ^ 1), (z_at >> 1) != (z_here >> 1))
        for mask, swap in zip(masks, swaps):
            mask[rows] = jnp.full((2 * part_rows, mask.shape[1]), jnp.where(swap, 1, 0), jnp.int32)
    for copy in copies:
        copy.wait()
    for shift in range(strata):
        to = (me + shift) & (strata - 1)
        out, share = messages[shift], messages[strata + shift]
        out[...] = own[pl.ds(pl.multiple_of(start_of(to), block_rows), block_rows), :]
        for k in range(PANELS):
            lo = k * part_rows
            at = pl.multiple_of(starts[k] + to * part_rows, part_rows)
            share[lo : lo + part_rows] = own[pl.ds(at, part_rows), :]


def pack_call(panel_order, row_block, kernel, samples):
    strata = lax.axis_size("cols")
    rows, right = samples.shape
    block_rows = rows // row_block.shape[0]
    size = PANELS * PW
    f32 = jnp.float32
    message = pltpu.VMEM((block_rows, size), f32)
    share = pltpu.VMEM((PANELS * (block_rows // strata), size), f32)
    mask = pltpu.VMEM((PANELS * 2 * (block_rows // strata), size), jnp.int32)
    *messages, picked, first, second = pl.pallas_call(
        pack_kernel,
        in_specs=[
            pl.BlockSpec(memory_space=pltpu.SMEM),
            pl.BlockSpec(memory_space=pltpu.SMEM),
            pl.BlockSpec(memory_space=pltpu.HBM),
            pl.BlockSpec(memory_space=pltpu.VMEM),
        ],
        out_shape=[message] * strata
        + [share] * strata
        + [pltpu.VMEM((PANELS, block_rows, right), f32), mask, mask],
        scratch_shapes=[pltpu.VMEM((rows, size), f32), pltpu.SemaphoreType.DMA((PANELS,))],
        cost_estimate=pl.CostEstimate(flops=0, bytes_accessed=2_000_000, transcendentals=0),
        compiler_params=pltpu.CompilerParams(vmem_limit_bytes=60 * 1024 * 1024),
        name="pack_messages",
    )(panel_order, row_block, kernel, samples)
    return messages[:strata], messages[strata:], picked, (first, second)


def shift_of(order_ref, k, axis, strata):
    per_place = lax.axis_size("rows") // strata
    if axis == "cols":
        return (lax.axis_index("cols") - lax.div(order_ref[k], per_place)) & (strata - 1)
    return ((lax.axis_index("rows") >> 4) - lax.div(lax.rem(order_ref[k], per_place), 4)) & 3


def piece_kernel(order_ref, *refs):
    got, out_ref = refs[:-1], refs[-1]
    for k in range(PANELS):
        columns = slice(k * PW, (k + 1) * PW)
        shift = shift_of(order_ref, k, "cols", len(got))
        for s, source in enumerate(got):

            @pl.when(shift == s)
            def _():
                out_ref[:, columns] = source[:, columns]


def share_kernel(order_ref, *refs):
    got, (right_ref, out_ref) = refs[:-2], refs[-2:]
    part_rows = right_ref.shape[1] // len(got)
    for k in range(PANELS):
        columns = slice(k * PW, (k + 1) * PW)
        lo = (2 * k + 1) * part_rows
        for chunk in range(len(got)):
            out_ref[lo : lo + part_rows, chunk * SIDE : (chunk + 1) * SIDE] = right_ref[
                k, chunk * part_rows : (chunk + 1) * part_rows
            ]
        shift = shift_of(order_ref, k, "cols", len(got))
        for s, source in enumerate(got):

            @pl.when(shift == s)
            def _():
                for p in range(PANELS):
                    out_ref[2 * p * part_rows : (2 * p + 1) * part_rows, columns] = source[
                        p * part_rows : (p + 1) * part_rows, columns
                    ]


def load_kernel(order_ref, *refs):
    got, out_ref = refs[:-1], refs[-1]
    rows = out_ref.shape[0] // PANELS
    for k in range(PANELS):
        at = slice(k * rows, (k + 1) * rows)
        shift = shift_of(order_ref, k, "rows", lax.axis_size("cols"))
        for s, source in enumerate(got):

            @pl.when(shift == s)
            def _():
                out_ref[at] = source[at]


def choose_call(body, panel_order, got, rows, name):
    return pl.pallas_call(
        body,
        in_specs=[pl.BlockSpec(memory_space=pltpu.SMEM)] + [pl.BlockSpec(memory_space=pltpu.VMEM)] * len(got),
        out_shape=jax.ShapeDtypeStruct((rows, PANELS * PW), jnp.float32),
        cost_estimate=pl.CostEstimate(flops=0, bytes_accessed=1_000_000, transcendentals=0),
        compiler_params=pltpu.CompilerParams(vmem_limit_bytes=16 * 1024 * 1024),
        name=name,
    )(panel_order, *got)


def on_device(kernel, row_block, panel_order, samples):
    rows_count, cols_count = lax.axis_size("rows"), lax.axis_size("cols")
    block_rows = kernel.shape[0] // row_block.shape[0]
    part_rows = block_rows // cols_count

    def along_y(array, shift):
        return lax.ppermute(
            array, "cols", [(i, (i + shift) % cols_count) for i in range(cols_count)]
        )

    def along_rows(array, move):
        pairs = []
        for r in range(rows_count):
            x, z, core = move(r // 16, r % 16 // 2, r % 2)
            pairs.append((r, x % 4 * 16 + z % 8 * 2 + core))
        return lax.ppermute(array, "rows", pairs)

    def along_x(array, shift):
        return along_rows(array, lambda x, z, c: (x + shift, z, c))

    def to_core(array):
        return along_rows(array, lambda x, z, c: (x, z, c ^ 1))

    messages, shares, right, masks = pack_call(panel_order, row_block, kernel, samples)
    got = messages[:1] + [along_y(messages[s], s) for s in range(1, cols_count)]
    piece = choose_call(piece_kernel, panel_order, got, block_rows, "choose_pieces")
    across = lax.all_gather(piece, "rows", axis=0, tiled=True)
    got = shares[:1] + [along_y(shares[s], s) for s in range(1, cols_count)]
    load = choose_call(share_kernel, panel_order, [*got, right], block_rows, "choose_shares")

    got = [load] + [along_x(load, s) for s in range(1, 4)]
    load = choose_call(load_kernel, panel_order, got, block_rows, "choose_along_x")
    other = along_rows(load, lambda x, z, c: (x, (z // 2 ^ 1) * 2 + z % 2, c))
    load = jnp.where(masks[0] != 0, other, load)
    other = along_rows(load, lambda x, z, c: (x, (3 - z // 2) * 2 + z % 2, c))
    load = jnp.where(masks[1] != 0, other, load)
    other = along_rows(load, lambda x, z, c: (x, z ^ 1, c))

    def part(array, first):
        at = [(2 * k + first) * part_rows for k in range(PANELS)]
        return [array[lo : lo + part_rows] for lo in at]

    shares = jnp.concatenate(part(load, 0) + part(other, 0), 0)
    rights = jnp.concatenate(part(load, 1) + part(other, 1), 0)
    load = jnp.concatenate([shares] + [along_y(shares, s) for s in range(1, cols_count)] + [rights], 0)
    other = to_core(load)
    load, piece = lax.optimization_barrier((load, piece))
    pieces = [piece] + [along_y(piece, s) for s in range(1, cols_count)]

    v1, rest, under, right = first_call(load, other)
    rest, under, *pieces = lax.optimization_barrier((rest, under, *pieces))
    v2, cross = second_call(rest, under)
    factor, weights, solved, reduced = apply_call(row_block, pieces, v1, cross, v2, right, samples)
    trailing = update_call(kernel, weights, across)
    return trailing, factor, solved, reduced


def solution(mesh):
    in_specs = (P("rows", "cols"), P("rows"), P(), P("rows", "cols"))
    out_specs = (P("rows", "cols"), P("rows", None), P(None, "cols"), P("rows", "cols"))
    return jax.shard_map(
        on_device, mesh=mesh, in_specs=in_specs, out_specs=out_specs, check_vma=False
    )
```

```python
import jax
import jax.numpy as jnp
from jax import lax
from jax.experimental import pallas as pl
from jax.experimental.pallas import tpu as pltpu
from jax.sharding import PartitionSpec as P

PW = 256
PANELS = 2
EXACT = lax.Precision.HIGHEST
SIDE = 128
STEP = 8


def dot_nt(a, b, precision=EXACT):
    return lax.dot_general(a, b, (((1,), (1,)), ((), ())), precision=precision, preferred_element_type=jnp.float32)


def dot_nn(a, b, precision=EXACT):
    return lax.dot_general(a, b, (((1,), (0,)), ((), ())), precision=precision, preferred_element_type=jnp.float32)


def lanes_of(rows, lane):
    return jnp.broadcast_to(rows[:, lane : lane + 1], (STEP, SIDE))


def sublanes_of(rows, sub):
    return jnp.broadcast_to(rows[sub : sub + 1, :], (STEP, SIDE))


def small_inverse(spread):
    inv, low = [None] * STEP, [[None] * STEP for _ in range(STEP)]
    rest = [list(r) for r in spread]
    for s in range(STEP):
        inv[s] = lax.rsqrt(rest[s][s])
        for r in range(s + 1, STEP):
            low[r][s] = rest[r][s] * inv[s]
        for r in range(s + 1, STEP):
            for q in range(s + 1, r + 1):
                rest[r][q] = rest[r][q] - low[r][s] * low[q][s]
    out = [[None] * STEP for _ in range(STEP)]
    for r in range(STEP):
        out[r][r] = inv[r]
        for s in range(r):
            total = low[r][s] * out[s][s]
            for q in range(s + 1, r):
                total = total + low[r][q] * out[q][s]
            out[r][s] = -inv[r] * total
    return out


def tile_inverse(d_ref, x_ref):
    groups = SIDE // STEP
    sub = lax.broadcasted_iota(jnp.int32, (STEP, SIDE), 0)
    lane = lax.broadcasted_iota(jnp.int32, (STEP, SIDE), 1)
    left = [d_ref[STEP * g : STEP * (g + 1), :] for g in range(groups)]
    right = [jnp.where(lane == sub + STEP * g, 1.0, 0.0).astype(jnp.float32) for g in range(groups)]
    for b in range(groups):
        here_l, here_r = left[b], right[b]
        cols = [lanes_of(here_l, STEP * b + s) for s in range(STEP)]
        spread = [[sublanes_of(cols[s], r) if s <= r else None for s in range(STEP)] for r in range(STEP)]
        v = small_inverse(spread)
        in_l = [sublanes_of(here_l, s) for s in range(STEP)]
        in_r = [sublanes_of(here_r, s) for s in range(STEP)]
        out_l, out_r = [], []
        for r in range(STEP):
            tl, tr = v[r][0] * in_l[0], v[r][0] * in_r[0]
            for s in range(1, r + 1):
                tl, tr = tl + v[r][s] * in_l[s], tr + v[r][s] * in_r[s]
            out_l.append(tl)
            out_r.append(tr)
        new_r = out_r[0]
        for r in range(1, STEP):
            new_r = jnp.where(sub == r, out_r[r], new_r)
        x_ref[STEP * b : STEP * (b + 1), :] = new_r
        if b + 1 == groups:
            break
        t_l, t_r = [], []
        for s in range(STEP):
            tl, tr = v[STEP - 1][s] * out_l[STEP - 1], v[STEP - 1][s] * out_r[STEP - 1]
            for r in range(s, STEP - 1):
                tl, tr = tl + v[r][s] * out_l[r], tr + v[r][s] * out_r[r]
            t_l.append(tl)
            t_r.append(tr)
        for g in range(b + 1, groups):
            c = [lanes_of(left[g], STEP * b + s) for s in range(STEP)]
            sl, sr = c[0] * t_l[0], c[0] * t_r[0]
            for s in range(1, STEP):
                sl, sr = sl + c[s] * t_l[s], sr + c[s] * t_r[s]
            left[g], right[g] = left[g] - sl, right[g] - sr


def halves(array):
    high = array.astype(jnp.bfloat16)
    return high, (array - high.astype(jnp.float32)).astype(jnp.bfloat16)


def two_tiles(a, v, d, x, beside=None):
    v[...] = jnp.zeros_like(v)

    @pl.loop(0, 2)
    def _(k):
        at = pl.multiple_of(k * SIDE, SIDE)
        d[...] = a[pl.ds(at, SIDE), pl.ds(at, SIDE)]
        tile_inverse(d, x)
        if beside is not None:
            beside(at)

        @pl.when(k == 0)
        def _():
            own = x[...]
            v[:SIDE, :SIDE] = own
            below = dot_nt(a[SIDE:, :SIDE], own)
            a[SIDE:, SIDE:] = a[SIDE:, SIDE:] - dot_nt(below, below)
            v[SIDE:, :SIDE] = -dot_nn(below, own)

        @pl.when(k == 1)
        def _():
            own = x[...]
            v[SIDE:, SIDE:] = own
            v[SIDE:, :SIDE] = dot_nn(own, v[SIDE:, :SIDE])


def first_kernel(own_ref, other_ref, v_ref, rest_ref, under_ref, right_ref, a, top, d, x):
    row_place, col_place = lax.axis_index("rows"), lax.axis_index("cols")
    core, odd = row_place & 1, (row_place >> 1) & 1
    strata = lax.axis_size("cols")
    share = own_ref.shape[0] // (strata + 1)
    part_rows = share // (2 * PANELS)
    block_rows = part_rows * strata
    for c, source in enumerate((own_ref, other_ref)):
        for z in range(2):
            member = (odd ^ z) * 2 + (core ^ c)
            for k in range(PANELS):
                base = k * PW + member * block_rows
                lo = (z * PANELS + k) * part_rows
                for shift in range(strata):
                    part = (col_place - shift) & (strata - 1)
                    at = pl.multiple_of(base + part * part_rows, part_rows)
                    a[pl.ds(at, part_rows), :] = source[shift * share + lo : shift * share + lo + part_rows, :]
                for chunk in range(block_rows // part_rows):
                    at = pl.multiple_of(base + chunk * part_rows, part_rows)
                    right_ref[pl.ds(at, part_rows), :] = source[
                        strata * share + lo : strata * share + lo + part_rows, chunk * SIDE : (chunk + 1) * SIDE
                    ]
    top[...] = a[:PW, :PW]
    two_tiles(top, v_ref, d, x)
    v = v_ref[...]
    low = dot_nt(a[PW:, :PW], v)
    rest_ref[...] = a[PW:, PW:] - dot_nt(low, low)
    under_ref[...] = -dot_nn(low, v)


def square(side):
    return jax.ShapeDtypeStruct((side, side), jnp.float32)


def first_call(own, other):
    right = jax.ShapeDtypeStruct((PANELS * PW, SIDE), jnp.float32)
    return pl.pallas_call(
        first_kernel,
        out_shape=[square(PW), square(PW), square(PW), right],
        scratch_shapes=[
            pltpu.VMEM((PANELS * PW, PANELS * PW), jnp.float32),
            pltpu.VMEM((PW, PW), jnp.float32),
            pltpu.VMEM((SIDE, SIDE), jnp.float32),
            pltpu.VMEM((SIDE, SIDE), jnp.float32),
        ],
        cost_estimate=pl.CostEstimate(flops=12_000_000_000, bytes_accessed=2_000_000, transcendentals=0),
        compiler_params=pltpu.CompilerParams(vmem_limit_bytes=16 * 1024 * 1024),
        name="eliminate_first",
    )(own, other)


def second_kernel(block_ref, *refs):
    pieces, refs = refs[:-16], refs[-16:]
    v1_ref, rest_ref, under_ref, rc_ref, ri_ref, f_ref, w_ref, y_ref, r_ref, a, v2_ref, d, x, p, t, s_ref = refs
    me = lax.axis_index("cols")
    rows_count = lax.axis_size("rows")
    block_rows = pieces[0].shape[0]
    for u in range(len(pieces)):
        shift = (me - lax.div(block_ref[u], rows_count)) & (len(pieces) - 1)
        for s, piece in enumerate(pieces):

            @pl.when(shift == s)
            def _():
                p[u * block_rows : (u + 1) * block_rows] = piece[...]

    def beside(at):
        rows = pl.ds(at, SIDE)
        p1, v1 = p[rows, :PW], v1_ref[...]
        f1 = dot_nt(p1, v1)
        f_ref[rows, :PW] = f1
        w_ref[rows, :PW] = dot_nn(f1, v1)
        t[rows, :] = p[rows, PW:] + dot_nt(p1, under_ref[...])
        y_ref[rows, :] = dot_nn(v1_ref[rows, :], rc_ref[:PW])
        s_ref[rows, :] = rc_ref[pl.ds(PW + at, SIDE), :] + dot_nn(under_ref[rows, :], rc_ref[:PW])

    a[...] = rest_ref[...]
    two_tiles(a, v2_ref, d, x, beside)
    v2 = v2_ref[...]
    f2 = dot_nt(t[...], v2)
    f_ref[:, PW:] = f2
    w2 = dot_nn(f2, v2)
    w_ref[:, PW:] = w2
    w_ref[:, :PW] = w_ref[:, :PW] + dot_nn(w2, under_ref[...])
    y2 = dot_nn(v2, s_ref[...])
    y_ref[PW:] = y2
    r_ref[...] = ri_ref[...] - dot_nn(f_ref[:, :PW], y_ref[:PW]) - dot_nn(f2, y2)


def second_call(row_block, pieces, v1, rest, under, rc, ri):
    size, right = rc.shape
    rows = ri.shape[0]
    f32 = jnp.float32
    operands = (*pieces, v1, rest, under, rc, ri)
    return pl.pallas_call(
        second_kernel,
        in_specs=[pl.BlockSpec(memory_space=pltpu.SMEM)]
        + [pl.BlockSpec(memory_space=pltpu.VMEM)] * len(operands),
        out_shape=[
            jax.ShapeDtypeStruct((rows, size), f32),
            jax.ShapeDtypeStruct((rows, size), f32),
            jax.ShapeDtypeStruct((size, right), f32),
            jax.ShapeDtypeStruct((rows, right), f32),
        ],
        scratch_shapes=[
            pltpu.VMEM((PW, PW), f32),
            pltpu.VMEM((PW, PW), f32),
            pltpu.VMEM((SIDE, SIDE), f32),
            pltpu.VMEM((SIDE, SIDE), f32),
            pltpu.VMEM((rows, size), f32),
            pltpu.VMEM((rows, PW), f32),
            pltpu.VMEM((PW, right), f32),
        ],
        cost_estimate=pl.CostEstimate(flops=16_000_000_000, bytes_accessed=4_000_000, transcendentals=0),
        compiler_params=pltpu.CompilerParams(vmem_limit_bytes=16 * 1024 * 1024),
        name="eliminate_second",
    )(row_block, *operands)


WIDTH = 1024


def update_kernel(k_ref, w_ref, b_ref, o_ref, held, gathered, out, k_sems, b_sems, out_sems):
    cols = k_ref.shape[1]
    parts = [slice(i * WIDTH, (i + 1) * WIDTH) for i in range(cols // WIDTH)]
    b_loads = [pltpu.make_async_copy(b_ref.at[at], gathered.at[at], b_sems.at[i]) for i, at in enumerate(parts)]
    k_loads = [pltpu.make_async_copy(k_ref.at[:, at], held.at[:, at], k_sems.at[i]) for i, at in enumerate(parts)]
    for b_load, k_load in zip(b_loads, k_loads):
        b_load.start()
        k_load.start()
    rows = w_ref.shape[0]
    wh, wl = halves(w_ref[...])
    both = jnp.concatenate([wh, wl], 0)
    stores = []
    for i, at in enumerate(parts):
        b_loads[i].wait()
        top, bottom = halves(gathered[at])
        wide = dot_nt(both, top, None)
        total = wide[:rows] + wide[rows:] + dot_nt(wh, bottom, None)
        k_loads[i].wait()
        out[:, at] = held[:, at] - total
        stores.append(pltpu.make_async_copy(out.at[:, at], o_ref.at[:, at], out_sems.at[i]))
        stores[-1].start()
    for store in stores:
        store.wait()


def update_call(kernel, weights, across):
    rows, cols = kernel.shape
    size = weights.shape[1]
    count = cols // WIDTH
    f32 = jnp.float32
    return pl.pallas_call(
        update_kernel,
        in_specs=[
            pl.BlockSpec(memory_space=pltpu.HBM),
            pl.BlockSpec(memory_space=pltpu.VMEM),
            pl.BlockSpec(memory_space=pltpu.HBM),
        ],
        out_specs=pl.BlockSpec(memory_space=pltpu.HBM),
        out_shape=jax.ShapeDtypeStruct((rows, cols), f32),
        scratch_shapes=[
            pltpu.VMEM((rows, cols), f32),
            pltpu.VMEM((cols, size), f32),
            pltpu.VMEM((rows, cols), f32),
            pltpu.SemaphoreType.DMA((count,)),
            pltpu.SemaphoreType.DMA((count,)),
            pltpu.SemaphoreType.DMA((count,)),
        ],
        cost_estimate=pl.CostEstimate(flops=6 * rows * cols * size, bytes_accessed=16_000_000, transcendentals=0),
        compiler_params=pltpu.CompilerParams(vmem_limit_bytes=50 * 1024 * 1024),
        name="trailing_update",
    )(kernel, weights, across)


def pack_kernel(order_ref, block_ref, kernel_ref, samples_ref, *rest):
    messages, right_ref, masks, own, sems = rest[:-5], rest[-5], rest[-4:-2], rest[-2], rest[-1]
    strata = len(messages) // 2
    me = lax.axis_index("cols")
    local_cols = kernel_ref.shape[1]
    blocks_here = strata
    block_rows = kernel_ref.shape[0] // blocks_here
    part_rows = block_rows // strata
    per_place = local_cols // PW
    copies = []
    for k in range(PANELS):
        at = pl.multiple_of(lax.rem(order_ref[k], per_place) * PW, PW)
        copies.append(
            pltpu.make_async_copy(
                kernel_ref.at[:, pl.ds(at, PW)], own.at[:, k * PW : (k + 1) * PW], sems.at[k]
            )
        )
        copies[-1].start()
    rows_count = lax.axis_size("rows")

    def start_of(stratum):
        slot = jnp.int32(0)
        for u in range(blocks_here):
            slot = jnp.where(lax.div(block_ref[u], rows_count) == stratum, u, slot)
        return slot * block_rows

    starts = [start_of(lax.div(order_ref[k], per_place)) for k in range(PANELS)]
    for k in range(PANELS):
        right_ref[k] = samples_ref[pl.ds(pl.multiple_of(starts[k], block_rows), block_rows), :]
    z_here = (lax.axis_index("rows") >> 2) & 3
    for k in range(PANELS):
        z_at = lax.rem(order_ref[k], 4)
        rows = slice(k * 2 * part_rows, (k + 1) * 2 * part_rows)
        swaps = (z_at == (z_here ^ 1), (z_at >> 1) != (z_here >> 1))
        for mask, swap in zip(masks, swaps):
            mask[rows] = jnp.full((2 * part_rows, mask.shape[1]), jnp.where(swap, 1, 0), jnp.int32)
    for copy in copies:
        copy.wait()
    for shift in range(strata):
        to = (me + shift) & (strata - 1)
        out, share = messages[shift], messages[strata + shift]
        out[...] = own[pl.ds(pl.multiple_of(start_of(to), block_rows), block_rows), :]
        for k in range(PANELS):
            lo = k * part_rows
            at = pl.multiple_of(starts[k] + to * part_rows, part_rows)
            share[lo : lo + part_rows] = own[pl.ds(at, part_rows), :]


def pack_call(panel_order, row_block, kernel, samples):
    strata = lax.axis_size("cols")
    rows, right = samples.shape
    block_rows = rows // row_block.shape[0]
    size = PANELS * PW
    f32 = jnp.float32
    message = pltpu.VMEM((block_rows, size), f32)
    share = pltpu.VMEM((PANELS * (block_rows // strata), size), f32)
    mask = pltpu.VMEM((PANELS * 2 * (block_rows // strata), size), jnp.int32)
    *messages, picked, first, second = pl.pallas_call(
        pack_kernel,
        in_specs=[
            pl.BlockSpec(memory_space=pltpu.SMEM),
            pl.BlockSpec(memory_space=pltpu.SMEM),
            pl.BlockSpec(memory_space=pltpu.HBM),
            pl.BlockSpec(memory_space=pltpu.VMEM),
        ],
        out_shape=[message] * strata
        + [share] * strata
        + [pltpu.VMEM((PANELS, block_rows, right), f32), mask, mask],
        scratch_shapes=[pltpu.VMEM((rows, size), f32), pltpu.SemaphoreType.DMA((PANELS,))],
        cost_estimate=pl.CostEstimate(flops=0, bytes_accessed=2_000_000, transcendentals=0),
        compiler_params=pltpu.CompilerParams(vmem_limit_bytes=60 * 1024 * 1024),
        name="pack_messages",
    )(panel_order, row_block, kernel, samples)
    return messages[:strata], messages[strata:], picked, (first, second)


def shift_of(order_ref, k, axis, strata):
    per_place = lax.axis_size("rows") // strata
    if axis == "cols":
        return (lax.axis_index("cols") - lax.div(order_ref[k], per_place)) & (strata - 1)
    return ((lax.axis_index("rows") >> 4) - lax.div(lax.rem(order_ref[k], per_place), 4)) & 3


def piece_kernel(order_ref, *refs):
    got, out_ref = refs[:-1], refs[-1]
    for k in range(PANELS):
        columns = slice(k * PW, (k + 1) * PW)
        shift = shift_of(order_ref, k, "cols", len(got))
        for s, source in enumerate(got):

            @pl.when(shift == s)
            def _():
                out_ref[:, columns] = source[:, columns]


def share_kernel(order_ref, *refs):
    got, (right_ref, out_ref) = refs[:-2], refs[-2:]
    part_rows = right_ref.shape[1] // len(got)
    for k in range(PANELS):
        columns = slice(k * PW, (k + 1) * PW)
        lo = (2 * k + 1) * part_rows
        for chunk in range(len(got)):
            out_ref[lo : lo + part_rows, chunk * SIDE : (chunk + 1) * SIDE] = right_ref[
                k, chunk * part_rows : (chunk + 1) * part_rows
            ]
        shift = shift_of(order_ref, k, "cols", len(got))
        for s, source in enumerate(got):

            @pl.when(shift == s)
            def _():
                for p in range(PANELS):
                    out_ref[2 * p * part_rows : (2 * p + 1) * part_rows, columns] = source[
                        p * part_rows : (p + 1) * part_rows, columns
                    ]


def load_kernel(order_ref, *refs):
    got, out_ref = refs[:-1], refs[-1]
    rows = out_ref.shape[0] // PANELS
    for k in range(PANELS):
        at = slice(k * rows, (k + 1) * rows)
        shift = shift_of(order_ref, k, "rows", lax.axis_size("cols"))
        for s, source in enumerate(got):

            @pl.when(shift == s)
            def _():
                out_ref[at] = source[at]


def choose_call(body, panel_order, got, rows, name):
    return pl.pallas_call(
        body,
        in_specs=[pl.BlockSpec(memory_space=pltpu.SMEM)] + [pl.BlockSpec(memory_space=pltpu.VMEM)] * len(got),
        out_shape=jax.ShapeDtypeStruct((rows, PANELS * PW), jnp.float32),
        cost_estimate=pl.CostEstimate(flops=0, bytes_accessed=1_000_000, transcendentals=0),
        compiler_params=pltpu.CompilerParams(vmem_limit_bytes=16 * 1024 * 1024),
        name=name,
    )(panel_order, *got)


def on_device(kernel, row_block, panel_order, samples):
    rows_count, cols_count = lax.axis_size("rows"), lax.axis_size("cols")
    block_rows = kernel.shape[0] // row_block.shape[0]
    part_rows = block_rows // cols_count

    def along_y(array, shift):
        return lax.ppermute(
            array, "cols", [(i, (i + shift) % cols_count) for i in range(cols_count)]
        )

    def along_rows(array, move):
        pairs = []
        for r in range(rows_count):
            x, z, core = move(r // 16, r % 16 // 2, r % 2)
            pairs.append((r, x % 4 * 16 + z % 8 * 2 + core))
        return lax.ppermute(array, "rows", pairs)

    def along_x(array, shift):
        return along_rows(array, lambda x, z, c: (x + shift, z, c))

    def to_core(array):
        return along_rows(array, lambda x, z, c: (x, z, c ^ 1))

    messages, shares, right, masks = pack_call(panel_order, row_block, kernel, samples)
    got = messages[:1] + [along_y(messages[s], s) for s in range(1, cols_count)]
    piece = choose_call(piece_kernel, panel_order, got, block_rows, "choose_pieces")
    across = lax.all_gather(piece, "rows", axis=0, tiled=True)
    got = shares[:1] + [along_y(shares[s], s) for s in range(1, cols_count)]
    load = choose_call(share_kernel, panel_order, [*got, right], block_rows, "choose_shares")

    got = [load] + [along_x(load, s) for s in range(1, 4)]
    load = choose_call(load_kernel, panel_order, got, block_rows, "choose_along_x")
    other = along_rows(load, lambda x, z, c: (x, (z // 2 ^ 1) * 2 + z % 2, c))
    load = jnp.where(masks[0] != 0, other, load)
    other = along_rows(load, lambda x, z, c: (x, (3 - z // 2) * 2 + z % 2, c))
    load = jnp.where(masks[1] != 0, other, load)
    other = along_rows(load, lambda x, z, c: (x, z ^ 1, c))

    def part(array, first):
        at = [(2 * k + first) * part_rows for k in range(PANELS)]
        return [array[lo : lo + part_rows] for lo in at]

    shares = jnp.concatenate(part(load, 0) + part(other, 0), 0)
    rights = jnp.concatenate(part(load, 1) + part(other, 1), 0)
    load = jnp.concatenate([shares] + [along_y(shares, s) for s in range(1, cols_count)] + [rights], 0)
    other = to_core(load)
    load, piece = lax.optimization_barrier((load, piece))
    pieces = [piece] + [along_y(piece, s) for s in range(1, cols_count)]

    v1, rest, under, right = first_call(load, other)
    rest, under, *pieces = lax.optimization_barrier((rest, under, *pieces))
    factor, weights, solved, reduced = second_call(row_block, pieces, v1, rest, under, right, samples)
    trailing = update_call(kernel, weights, across)
    return trailing, factor, solved, reduced


def solution(mesh):
    in_specs = (P("rows", "cols"), P("rows"), P(), P("rows", "cols"))
    out_specs = (P("rows", "cols"), P("rows", None), P(None, "cols"), P("rows", "cols"))
    return jax.shard_map(
        on_device, mesh=mesh, in_specs=in_specs, out_specs=out_specs, check_vma=False
    )
```
